32 devices in a mesh: dp: 4 (over y, x), tile: 8 (over z, core).
Axes of the slice: x: 2, y: 2, z: 4, core: 2. Of those that a mesh axis runs over, the one named last changes fastest.
Arguments:
- features: bfloat16 [4, 64, 64, 128], P('dp', None, 'tile'), may hold values from -6 to 6
- occupied_block_mask: int32 [4, 8, 2], P('dp', 'tile'), may hold values 0 or 1
- conv_one: bfloat16 [27, 64, 64], replicated, may hold values from -0.15625 to 0.15625
- conv_two: bfloat16 [27, 64, 64], replicated, may hold values from -0.15625 to 0.15625
- gain: float32 [64], replicated, may hold values from 0.5 to 1.5
- shift: float32 [64], replicated, may hold values from -3 to 3
- cotangent: bfloat16 [4, 64, 64, 128], P('dp', None, 'tile'), may hold values from -6 to 6
Outputs:
- section_out: bfloat16 [4, 64, 64, 128], P('dp', None, 'tile')
- input_grad: bfloat16 [4, 64, 64, 128], P('dp', None, 'tile')
- grad_one: float32 [27, 64, 64], replicated
- grad_two: float32 [27, 64, 64], replicated
- gain_grad: float32 [64], replicated
- shift_grad: float32 [64], replicated
The draws below stay inside these ranges and needn't reach their ends.
Inputs may be any that keep to these rules, and one draw needn't show every extreme that they name: `occupied_block_mask`: each entry marks whether a block holds points.
All inputs are finite; a program needn't handle non-finite values.
Results may differ from the reference program's by a relative error of at most 0.0034.
Values may be sent and summed in bfloat16 or wider, within the bound.
A program may use at most 128 MiB of HBM per device.

```python
import jax
import jax.numpy as jnp
from jax import lax

CH = 64
BLK = 8
TAPS = 27
YB = 2
SCENES = 4
NXB = 8
NX = 64
HY = 128


def touch_ends(array, rng, least, top_value):
    place = [jax.random.randint(jax.random.fold_in(rng, axis), (), 0, length) for axis, length in enumerate(array.shape)]
    main_axis = array.shape.index(max(array.shape))
    neighbour = place[:main_axis] + [(place[main_axis] + 1) % array.shape[main_axis]] + place[main_axis + 1:]
    return array.at[tuple(place)].set(least).at[tuple(neighbour)].set(top_value)


def steps_of(key, dims, shards, least, high):
    level = 1.0
    for position, shards_of in shards:
        steps = jax.random.uniform(jax.random.fold_in(jax.random.fold_in(key, 6), position), (shards_of,), jnp.float32, least / len(shards), high / len(shards))
        level = level * jnp.repeat(jnp.exp(steps), dims[position] // shards_of).reshape((-1,) + (1,) * (len(dims) - 1 - position))
    return level


def noise(rng, shape, width, limit, shards=(), dtype=jnp.bfloat16):
    drawn = width * jax.random.normal(rng, shape, jnp.float32)
    if shards:
        drawn = drawn * steps_of(rng, shape, shards, -0.22, 0.18)
    return jnp.clip(drawn, -limit, limit).astype(dtype)


def setup_inputs(seed: int = 0) -> dict:
    keys = jax.random.split(jax.random.key(seed), 8)
    features = noise(keys[0], (SCENES, CH, NX, HY), 1.0, 6.0, ((0, 4), (2, 8)))
    occupied_block_mask = touch_ends((jax.random.randint(keys[1], (SCENES, NXB, YB), 0, 4) < 3).astype(jnp.int32), jax.random.fold_in(keys[1], 1), 0, 1)
    conv_one = noise(keys[2], (TAPS, CH, CH), (TAPS * CH) ** -0.5, 0.15625)
    conv_two = noise(keys[3], (TAPS, CH, CH), (TAPS * CH) ** -0.5, 0.15625)
    gain = jnp.clip(1.0 + 0.1 * jax.random.normal(keys[4], (CH,), jnp.float32), 0.5, 1.5)
    shift = noise(keys[5], (CH,), 0.5, 3.0, (), jnp.float32)
    cotangent = noise(keys[6], (SCENES, CH, NX, HY), 1.0, 6.0, ((0, 4), (2, 8)))
    return {"features": features, "occupied_block_mask": occupied_block_mask, "conv_one": conv_one, "conv_two": conv_two, "gain": gain, "shift": shift, "cotangent": cotangent}


epsilon = 1e-05

def voxel_mask(occupied_block_mask, block_edge):
    scenes_here, x_blocks, y_blocks = occupied_block_mask.shape
    grown = jnp.broadcast_to(occupied_block_mask[:, :, None, None, :, None], (scenes_here, x_blocks, block_edge, block_edge, y_blocks, block_edge))
    return grown.reshape(scenes_here, 1, x_blocks * block_edge, block_edge * y_blocks * block_edge)

def widen(padded_x, height):
    scenes_here, channels, x_size, flat_size = padded_x.shape
    shaped = padded_x.reshape(scenes_here, channels, x_size, height, flat_size // height)
    return jnp.pad(shaped, ((0, 0), (0, 0), (0, 0), (1, 1), (1, 1)))

def window_rows(padded_grid, offset_x, offset_h):
    scenes_here, channels, x_pad, h_pad, y_pad = padded_grid.shape
    x_span, h_span, y_span = (x_pad - 2, h_pad - 2, y_pad - 2)
    pieces = [padded_grid[:, :, offset_x:offset_x + x_span, offset_h:offset_h + h_span, offset_y:offset_y + y_span] for offset_y in range(3)]
    return jnp.concatenate(pieces, axis=1).reshape(scenes_here, 3 * channels, x_span * h_span * y_span)

def convolve_one(padded_grid, weight):
    running = None
    for offset_x in range(3):
        for offset_h in range(3):
            column_matrix = window_rows(padded_grid, offset_x, offset_h).astype(jnp.float32)
            kernel_tap_block = weight[9 * offset_x + 3 * offset_h:9 * offset_x + 3 * offset_h + 3].reshape(-1, weight.shape[2]).astype(jnp.float32)
            matrix_product = jnp.einsum('zl,pzh->plh', kernel_tap_block, column_matrix, precision=lax.Precision.HIGHEST)
            running = matrix_product if running is None else running + matrix_product
    return running

def kernel_grad_one(padded_grid, delta_row_matrix):
    pieces = []
    for offset_x in range(3):
        for offset_h in range(3):
            column_matrix = window_rows(padded_grid, offset_x, offset_h).astype(jnp.float32)
            matrix_product = jnp.einsum('uzh,uih->zi', column_matrix, delta_row_matrix.astype(jnp.float32), precision=lax.Precision.HIGHEST)
            pieces.append(matrix_product.reshape(3, -1, matrix_product.shape[1]))
    return jnp.concatenate(pieces, axis=0)

def flipped(weight):
    return jnp.transpose(weight[::-1], (0, 2, 1))

def convolve_all(padded_grid, weight, shape_out):
    result = lax.map(lambda one_grid: convolve_one(one_grid[None], weight)[0], padded_grid)
    return result.reshape(shape_out)

def kernel_gradient_total(padded_grid, delta_row_matrix):
    per_scene = lax.map(lambda pair: kernel_grad_one(pair[0][None], pair[1][None]), (padded_grid, delta_row_matrix))
    return lax.optimization_barrier(jnp.sum(per_scene, axis=0))

def pad_x(array_in):
    return jnp.pad(array_in, ((0, 0), (0, 0), (1, 1), (0, 0)))

def reference(features, occupied_block_mask, conv_one, conv_two, gain, shift, cotangent):
    shape_out = features.shape
    scenes_all, channels = (shape_out[0], shape_out[1])
    vox_mask = voxel_mask(occupied_block_mask, BLK).astype(jnp.bfloat16)
    mask_f = vox_mask.astype(jnp.float32)
    inputs = features * vox_mask
    x_grid = widen(pad_x(inputs), BLK)
    pre_one = convolve_all(x_grid, conv_one, shape_out)
    active_count = jnp.sum(mask_f) * 1.0
    bn_mean = lax.optimization_barrier(jnp.sum(pre_one * mask_f, axis=(0, 2, 3))) / active_count
    centered = (pre_one - bn_mean[None, :, None, None]) * mask_f
    variance = lax.optimization_barrier(jnp.sum(centered * centered, axis=(0, 2, 3))) / active_count
    inv_std = lax.rsqrt(variance + epsilon)
    normal = (pre_one - bn_mean[None, :, None, None]) * inv_std[None, :, None, None]
    pre_act = gain[None, :, None, None] * normal + shift[None, :, None, None]
    act = (jax.nn.silu(pre_act) * mask_f).astype(jnp.bfloat16)
    a_grid = widen(pad_x(act), BLK)
    pre_two = convolve_all(a_grid, conv_two, shape_out)
    section_out = ((inputs.astype(jnp.float32) + pre_two) * mask_f).astype(jnp.bfloat16)
    delta_out = cotangent * vox_mask
    grad_two = kernel_gradient_total(a_grid, delta_out.reshape(scenes_all, channels, -1))
    d_grid = widen(pad_x(delta_out), BLK)
    activation_gradient = convolve_all(d_grid, flipped(conv_two), shape_out)
    sigmoid_z = jax.nn.sigmoid(pre_act)
    z_grad = activation_gradient * mask_f * sigmoid_z * (1.0 + pre_act * (1.0 - sigmoid_z))
    shift_grad = lax.optimization_barrier(jnp.sum(z_grad, axis=(0, 2, 3)))
    gain_grad = lax.optimization_barrier(jnp.sum(z_grad * normal, axis=(0, 2, 3)))
    scale_c = (gain * inv_std)[None, :, None, None]
    first_delta_gradient = (scale_c * (z_grad - (shift_grad / active_count)[None, :, None, None] - normal * (gain_grad / active_count)[None, :, None, None]) * mask_f).astype(jnp.bfloat16)
    grad_one = kernel_gradient_total(x_grid, first_delta_gradient.reshape(scenes_all, channels, -1))
    i_grid = widen(pad_x(first_delta_gradient), BLK)
    back_in = convolve_all(i_grid, flipped(conv_one), shape_out)
    input_grad = ((delta_out.astype(jnp.float32) + back_in) * mask_f).astype(jnp.bfloat16)
    return (section_out, input_grad, grad_one, grad_two, gain_grad, shift_grad)
```

```python
import functools

import jax
import jax.numpy as jnp
from jax import lax
from jax.experimental import pallas as pl
from jax.experimental.pallas import tpu as pltpu
from jax.sharding import PartitionSpec as P

BLK = 8
LANES = 128
EPSILON = 1e-05
MESH = pl.DeviceIdType.MESH
F32 = jnp.float32
BF16 = jnp.bfloat16


def kernel(
    n_dp, n_tile, ch, nx, hy,
    xd_ref, occ_ref, k1_ref, k2_ref, gain_ref, shift_ref,
    so_ref, ig_ref, q4, sums_out,
    w1_ref, w2_ref, w1f_ref, w2f_ref, xd_pad, a_pad, i_pad, s_x, s_d, s_t, d3, ar, part, rp, half, r1,
    halo_s, halo_r, ar_s, ar_r, rs_s, rs_r,
):
    n_z = n_tile // 2
    n_chips, n_all = n_dp * n_z, n_dp * n_tile
    dp, tile = lax.axis_index("dp"), lax.axis_index("tile")
    core, z = lax.rem(tile, 2), tile // 2
    me, chip = dp * n_tile + tile, dp * n_z + z
    flat = nx * hy
    rows_half = half.shape[1]
    size = r1.shape[2]
    owners = rows_half // size

    def each(count, body):
        def step(k, carry):
            body(k)
            return carry
        lax.fori_loop(1, count, step, 0, unroll=count <= 32)

    def peer(k):
        other = lax.rem(me + k, n_all)
        return (other // n_tile, lax.rem(other, n_tile))

    def chip_peer(k):
        other = lax.rem(chip + k, n_chips)
        return other, (other // n_z, lax.rem(other, n_z) * 2 + core)

    sibling = (dp, z * 2 + 1 - core)
    has_left, has_right = tile > 0, tile < n_tile - 1

    barrier = pltpu.get_barrier_semaphore()
    each(n_all, lambda k: pl.semaphore_signal(
        barrier, inc=1, device_id=peer(k), device_id_type=MESH))

    width = hy // BLK
    spot = lax.broadcasted_iota(jnp.int32, (1, flat), 1)
    block_x, block_y = spot // (hy * BLK), lax.rem(spot, width) // BLK
    mask = jnp.zeros((1, flat), F32)
    for bx in range(nx // BLK):
        for by in range(width // BLK):
            mask = jnp.where((block_x == bx) & (block_y == by),
                             occ_ref[bx, by].astype(F32), mask)
    xd_pad[:, pl.ds(hy, flat)] = (xd_ref[...].astype(F32) * mask).astype(BF16)
    same = (lax.broadcasted_iota(jnp.int32, (ch, ch), 0)
            == lax.broadcasted_iota(jnp.int32, (ch, ch), 1)).astype(BF16)

    def as_matrix(taps, out):
        for a in range(3):
            out[pl.ds(a * ch, ch), :] = lax.dot_general(
                same, taps[pl.ds(a * 9 * ch, 9 * ch), :], (((1,), (1,)), ((), ())),
                preferred_element_type=F32).astype(BF16)

    def as_flipped(taps, out):
        for a in range(3):
            out[pl.ds(a * ch, ch), :] = jnp.concatenate(
                [taps[pl.ds((26 - 9 * a - k) * ch, ch), :] for k in range(9)], axis=1)

    as_matrix(k1_ref, w1_ref)

    pl.semaphore_wait(barrier, n_all - 1)

    def halo(phase, src, first, pad):
        low = pltpu.make_async_remote_copy(
            src_ref=src.at[:, pl.ds(first, hy)],
            dst_ref=pad.at[:, pl.ds(flat + hy, hy)],
            send_sem=halo_s.at[phase, 0], recv_sem=halo_r.at[phase, 0],
            device_id=(dp, tile - 1), device_id_type=MESH)
        high = pltpu.make_async_remote_copy(
            src_ref=src.at[:, pl.ds(first + flat - hy, hy)],
            dst_ref=pad.at[:, pl.ds(0, hy)],
            send_sem=halo_s.at[phase, 1], recv_sem=halo_r.at[phase, 1],
            device_id=(dp, tile + 1), device_id_type=MESH)

        @pl.when(has_left)
        def _():
            low.start()

        @pl.when(has_right)
        def _():
            high.start()

        def finish():
            @pl.when(has_left)
            def _():
                low.wait_send()
                high.wait_recv()

            @pl.when(has_right)
            def _():
                high.wait_send()
                low.wait_recv()

        return finish

    def zero_ends(pad):
        @pl.when(jnp.logical_not(has_left))
        def _():
            pad[:, pl.ds(0, hy)] = jnp.zeros((pad.shape[0], hy), pad.dtype)

        @pl.when(jnp.logical_not(has_right))
        def _():
            pad[:, pl.ds(flat + hy, hy)] = jnp.zeros((pad.shape[0], hy), pad.dtype)

    lane = lax.broadcasted_iota(jnp.int32, (1, hy), 1)
    row_h, row_y = lane // width, lax.rem(lane, width)

    def shifts(pad, first, out, inner=True, outer=True):
        def plane(x, carry):
            at = pl.ds(x * hy if isinstance(x, int) else pl.multiple_of(x * hy, hy), hy)
            values = pad[pl.ds(first, ch), at]
            for b in range(3):
                for c in range(3):
                    step = (b - 1) * width + (c - 1)
                    moved = values
                    if step:
                        moved = pltpu.roll(values, (-step) % hy, 1)
                        fits = ((row_h + (b - 1) >= 0) & (row_h + (b - 1) < BLK)
                                & (row_y + (c - 1) >= 0) & (row_y + (c - 1) < width))
                        moved = jnp.where(fits, moved, jnp.zeros_like(moved))
                    out[pl.ds((3 * b + c) * ch, ch), at] = moved.astype(BF16)
            return carry
        if inner:
            lax.fori_loop(1, nx + 1, plane, 0, unroll=True)
        if outer:
            plane(0, 0)
            plane(nx + 1, 0)

    def conv(weight, stack):
        grown = jnp.dot(weight[...], stack[...], preferred_element_type=F32)
        return (grown[:ch, :flat] + grown[ch:2 * ch, hy:hy + flat]
                + grown[2 * ch:, 2 * hy:2 * hy + flat])

    nt = (((1,), (1,)), ((), ()))
    used = 27 * ch // 2

    def grad_by_input(stack, g):
        rows = 9 * ch
        side = rows // 2
        part[g, pl.ds(0, rows), :] = lax.dot_general(
            stack[...], d3[pl.ds(0, 2 * ch), :], nt, preferred_element_type=F32)
        rest = lax.dot_general(
            stack[...], d3[pl.ds(2 * ch, ch), :], nt, preferred_element_type=F32)
        part[g, pl.ds(rows, side), :] = jnp.concatenate([rest[:side], rest[side:]], axis=1)

    def grad_by_output(stack, g):
        rows = 3 * ch
        side = rows // 2
        for m in range(4):
            part[g, pl.ds(m * rows, rows), :] = lax.dot_general(
                d3[...], stack[pl.ds(m * 2 * ch, 2 * ch), :], nt, preferred_element_type=F32)
        rest = lax.dot_general(
            d3[...], stack[pl.ds(8 * ch, ch), :], nt, preferred_element_type=F32)
        part[g, pl.ds(4 * rows, side), :] = jnp.concatenate([rest[:side], rest[side:]], axis=1)

    def put_d3(value):
        for a in range(3):
            d3[pl.ds(a * ch, ch), pl.ds(a * hy, flat)] = value

    def to_rows(columns):
        spot = lax.broadcasted_iota(jnp.int32, (ch, LANES), 1)
        block = jnp.zeros((ch, LANES), F32)
        for index, column in enumerate(columns):
            block = jnp.where(spot == index, column, block)
        return jnp.transpose(block)[:8]

    def to_columns(rows):
        return jnp.transpose(jnp.concatenate([rows, jnp.zeros((LANES - 8, ch), F32)], axis=0))

    def small_start(call, first, second, third):
        ar[call, me, 0:1, :] = jnp.concatenate([first, second], axis=1)
        ar[call, me, 1:2, :] = jnp.concatenate([third, third], axis=1)
        each(n_all, lambda k: pltpu.make_async_remote_copy(
            src_ref=ar.at[call, me], dst_ref=ar.at[call, me],
            send_sem=ar_s.at[call], recv_sem=ar_r.at[call],
            device_id=peer(k), device_id_type=MESH).start())

    def small_end(call):
        arrived = ar.at[call, pl.ds(0, n_all - 1)]
        pltpu.make_async_copy(arrived, arrived, ar_r.at[call]).wait()
        pltpu.make_async_copy(arrived, arrived, ar_s.at[call]).wait()
        return ar[call, :, 0, :], ar[call, :, 1, :]

    def merge_moments(sums_squares, counts):
        total = jnp.sum(sums_squares, axis=0, keepdims=True)
        count = jnp.sum(counts, axis=0, keepdims=True)
        off = (sums_squares / jnp.maximum(counts, 1.0) - total / jnp.maximum(count, 1.0))
        between = jnp.sum(counts * off * off, axis=0, keepdims=True)
        return jnp.concatenate(
            [total[:, :ch], total[:, ch:] + between[:, :ch], count[:, :ch],
             jnp.zeros((5, ch), F32)], axis=0)

    def scatter_core(g):
        theirs = pl.ds(pl.multiple_of((1 - core) * rows_half, rows_half), rows_half)
        copy = pltpu.make_async_remote_copy(
            src_ref=part.at[g, theirs, :], dst_ref=rp.at[g],
            send_sem=rs_s.at[g, 0], recv_sem=rs_r.at[g, 0],
            device_id=sibling, device_id_type=MESH)
        copy.start()
        return copy

    def settle(g, stage, ref):
        pltpu.make_async_copy(ref, ref, rs_r.at[g, stage]).wait()

    def drain(g, stage, ref):
        pltpu.make_async_copy(ref, ref, rs_s.at[g, stage]).wait()

    def scatter_chips(g, copy):
        copy.wait()
        mine = pl.ds(pl.multiple_of(core * rows_half, rows_half), rows_half)
        total = part[g, mine, :] + rp[g]
        rp[g] = total
        half[g] = total.astype(BF16)

        def send(k):
            other, device = chip_peer(k)

            @pl.when(other < owners)
            def _():
                pltpu.make_async_remote_copy(
                    src_ref=half.at[g, pl.ds(pl.multiple_of(other * size, size), size), :],
                    dst_ref=r1.at[g, k - 1],
                    send_sem=rs_s.at[g, 1], recv_sem=rs_r.at[g, 1],
                    device_id=device, device_id_type=MESH).start()

        each(n_chips, send)

    def gather_chips(g):
        @pl.when(chip < owners)
        def _():
            settle(g, 1, r1.at[g])
            total = rp[g, pl.ds(pl.multiple_of(chip * size, size), size), :]
            for k in range(n_chips - 1):
                total = total + r1[g, k].astype(F32)
            place = pl.ds(pl.multiple_of(core * rows_half + chip * size, size), size)
            q4[g, place, :] = total.astype(BF16)

            def send(k):
                _, device = chip_peer(k)
                pltpu.make_async_remote_copy(
                    src_ref=q4.at[g, place, :], dst_ref=q4.at[g, place, :],
                    send_sem=rs_s.at[g, 2], recv_sem=rs_r.at[g, 2],
                    device_id=device, device_id_type=MESH).start()

            each(n_chips, send)

    def gather_core(g):
        @pl.when(chip < owners)
        def _():
            settle(g, 2, half.at[g, pl.ds(0, (owners - 1) * size), :])
            drain(g, 1, half.at[g, pl.ds(0, (owners - 1) * size), :])
            drain(g, 2, r1.at[g])

        @pl.when(chip >= owners)
        def _():
            settle(g, 2, half.at[g])
            drain(g, 1, half.at[g])

        mine = pl.ds(pl.multiple_of(core * rows_half, rows_half), rows_half)
        copy = pltpu.make_async_remote_copy(
            src_ref=q4.at[g, mine, :], dst_ref=q4.at[g, mine, :],
            send_sem=rs_s.at[g, 3], recv_sem=rs_r.at[g, 3],
            device_id=sibling, device_id_type=MESH)
        copy.start()
        return copy

    end_xd = halo(0, xd_pad, hy, xd_pad)
    shifts(xd_pad, 0, s_x, outer=False)
    zero_ends(xd_pad)
    zero_ends(a_pad)
    zero_ends(i_pad)
    end_xd()

    shifts(xd_pad, 0, s_x, inner=False)
    pre = conv(w1_ref, s_x)
    count_here = jnp.sum(mask, axis=1, keepdims=True)
    sums_here = jnp.sum(pre * mask, axis=1, keepdims=True)
    off = (pre - sums_here / jnp.maximum(count_here, 1.0)) * mask
    squares_here = jnp.sum(off * off, axis=1, keepdims=True)
    rows = to_rows([sums_here, squares_here])
    small_start(0, rows[0:1], rows[1:2], jnp.broadcast_to(count_here, (1, ch)))

    shifts(xd_pad, ch, s_d)
    as_flipped(k2_ref, w2f_ref)
    act_grad = conv(w2f_ref, s_d)
    gain_shift = to_columns(jnp.concatenate(
        [gain_ref[...], shift_ref[...], jnp.zeros((6, ch), F32)], axis=0))
    d3[...] = jnp.zeros(d3.shape, d3.dtype)
    if part.shape[1] > used:
        for g in range(2):
            part[g, pl.ds(used, part.shape[1] - used), :] = jnp.zeros(
                (part.shape[1] - used, LANES), F32)
    as_matrix(k2_ref, w2_ref)
    as_flipped(k1_ref, w1f_ref)

    moments = to_columns(merge_moments(*small_end(0)))
    count = moments[:, 2:3]
    mean = moments[:, 0:1] / count
    inv_std = lax.rsqrt(moments[:, 1:2] / count + EPSILON)
    gain, shift = gain_shift[:, 0:1], gain_shift[:, 1:2]
    normal = (pre - mean) * inv_std
    pre_act = gain * normal + shift
    sg = 1.0 / (1.0 + jnp.exp(-pre_act))
    act = (pre_act * sg * mask).astype(BF16)
    a_pad[:, pl.ds(hy, flat)] = act
    end_act = halo(1, a_pad, hy, a_pad)
    z_grad = act_grad * mask * sg * (1.0 + pre_act * (1.0 - sg))
    shift_here = jnp.sum(z_grad, axis=1, keepdims=True)
    gain_here = jnp.sum(z_grad * normal, axis=1, keepdims=True)
    rows = to_rows([shift_here, gain_here])
    small_start(1, rows[0:1], rows[1:2], rows[0:1])

    put_d3(act)
    grad_by_output(s_d, 0)
    two = scatter_core(0)
    shifts(a_pad, 0, s_t, outer=False)
    scatter_chips(0, two)
    end_act()
    shifts(a_pad, 0, s_t, inner=False)
    pre_two = conv(w2_ref, s_t)
    so_ref[...] = ((xd_pad[pl.ds(0, ch), pl.ds(hy, flat)].astype(F32) + pre_two) * mask).astype(BF16)

    totals = jnp.sum(small_end(1)[0], axis=0, keepdims=True)
    totals = jnp.concatenate([totals[:, :ch], totals[:, ch:], jnp.zeros((6, ch), F32)], axis=0)
    sums_out[...] = totals
    totals = to_columns(totals)
    delta_one = (gain * inv_std * (
        z_grad - totals[:, 0:1] / count - normal * (totals[:, 1:2] / count)) * mask).astype(BF16)
    i_pad[:, pl.ds(hy, flat)] = delta_one
    end_delta = halo(2, i_pad, hy, i_pad)
    put_d3(delta_one)
    grad_by_input(s_x, 1)
    one = scatter_core(1)
    gather_chips(0)
    scatter_chips(1, one)
    shifts(i_pad, 0, s_t, outer=False)
    end_delta()
    shifts(i_pad, 0, s_t, inner=False)
    back = conv(w1f_ref, s_t)
    ig_ref[...] = ((xd_pad[pl.ds(ch, ch), pl.ds(hy, flat)].astype(F32) + back) * mask).astype(BF16)
    two = gather_core(0)
    gather_chips(1)
    one = gather_core(1)
    two.wait()
    one.wait()


def unpack(ch, so_in, ig_in, q4, sums, so_ref, ig_ref, g1_ref, g2_ref, gain_ref, shift_ref):
    rows = 9 * ch
    half = rows // 2
    for a in range(2):
        g1_ref[pl.ds(a * rows, rows), :] = q4[1, pl.ds(0, rows), pl.ds(a * ch, ch)].astype(F32)
    for side in range(2):
        g1_ref[pl.ds(2 * rows + side * half, half), :] = (
            q4[1, pl.ds(rows, half), pl.ds(side * ch, ch)].astype(F32))
    rows = 3 * ch
    half = rows // 2
    for a in range(3):
        for m in range(4):
            for side in range(2):
                g2_ref[pl.ds((26 - 9 * a - 2 * m - side) * ch, ch), :] = (
                    q4[0, pl.ds(m * rows + a * ch, ch), pl.ds(side * ch, ch)].astype(F32))
    step = ch // 2
    for part in range(6):
        side, row = part // 3, part % 3
        a, top = part // 2, part % 2
        g2_ref[pl.ds((18 - 9 * a) * ch + top * step, step), :] = (
            q4[0, pl.ds(4 * rows + row * step, step), pl.ds(side * ch, ch)].astype(F32))
    so_ref[...] = so_in[...]
    ig_ref[...] = ig_in[...]
    shift_ref[...] = sums[0:1, :]
    gain_ref[...] = sums[1:2, :]


def local(n_dp, n_tile, features, occupied, conv_one, conv_two, gain, shift, cotangent):
    scenes, ch, nx, hy = features.shape
    flat = nx * hy
    xd = jnp.concatenate([features.reshape(ch, flat), cotangent.reshape(ch, flat)], axis=0)
    n_chips, n_all = n_dp * n_tile // 2, n_dp * n_tile
    used = 27 * ch // 2
    size = -(-used // (2 * n_chips * 16)) * 16
    rows_half = -(-used // (2 * size)) * size
    rows = 2 * rows_half
    vmem = pl.BlockSpec(memory_space=pltpu.VMEM)
    dma = pltpu.SemaphoreType.DMA
    so, ig, q4, sums = pl.pallas_call(
        functools.partial(kernel, n_dp, n_tile, ch, nx, hy),
        out_shape=(
            jax.ShapeDtypeStruct((ch, flat), BF16),
            jax.ShapeDtypeStruct((ch, flat), BF16),
            jax.ShapeDtypeStruct((2, rows, LANES), BF16),
            jax.ShapeDtypeStruct((8, ch), F32),
        ),
        in_specs=[vmem, pl.BlockSpec(memory_space=pltpu.SMEM)] + [vmem] * 4,
        out_specs=[vmem] * 4,
        scratch_shapes=[
            pltpu.VMEM((3 * ch, 9 * ch), BF16),
            pltpu.VMEM((3 * ch, 9 * ch), BF16),
            pltpu.VMEM((3 * ch, 9 * ch), BF16),
            pltpu.VMEM((3 * ch, 9 * ch), BF16),
            pltpu.VMEM((2 * ch, flat + 2 * hy), BF16),
            pltpu.VMEM((ch, flat + 2 * hy), BF16),
            pltpu.VMEM((ch, flat + 2 * hy), BF16),
            pltpu.VMEM((9 * ch, flat + 2 * hy), BF16),
            pltpu.VMEM((9 * ch, flat + 2 * hy), BF16),
            pltpu.VMEM((9 * ch, flat + 2 * hy), BF16),
            pltpu.VMEM((3 * ch, flat + 2 * hy), BF16),
            pltpu.VMEM((2, n_all, 2, LANES), F32),
            pltpu.VMEM((2, rows, LANES), F32),
            pltpu.VMEM((2, rows_half, LANES), F32),
            pltpu.VMEM((2, rows_half, LANES), BF16),
            pltpu.VMEM((2, n_chips - 1, size, LANES), BF16),
            dma((3, 2)), dma((3, 2)),
            dma((2,)), dma((2,)),
            dma((2, 4)), dma((2, 4)),
        ],
        compiler_params=pltpu.CompilerParams(
            collective_id=0, has_side_effects=True, vmem_limit_bytes=48 * 2**20),
    )(
        xd, occupied[0], conv_one.reshape(27 * ch, ch), conv_two.reshape(27 * ch, ch),
        gain.reshape(1, ch), shift.reshape(1, ch),
    )
    planes = features.shape[1:]
    so, ig, g1, g2, gg, sg = pl.pallas_call(
        functools.partial(unpack, ch),
        out_shape=(
            jax.ShapeDtypeStruct(planes, BF16),
            jax.ShapeDtypeStruct(planes, BF16),
            jax.ShapeDtypeStruct((27 * ch, ch), F32),
            jax.ShapeDtypeStruct((27 * ch, ch), F32),
            jax.ShapeDtypeStruct((1, ch), F32),
            jax.ShapeDtypeStruct((1, ch), F32),
        ),
        in_specs=[vmem] * 4,
        out_specs=[vmem] * 6,
        compiler_params=pltpu.CompilerParams(vmem_limit_bytes=16 * 2**20),
    )(so.reshape(planes), ig.reshape(planes), q4, sums)
    shape = features.shape
    return (so.reshape(shape), ig.reshape(shape), g1.reshape(27, ch, ch),
            g2.reshape(27, ch, ch), gg.reshape(ch), sg.reshape(ch))


def solution(mesh):
    split = P("dp", None, "tile", None)
    return jax.shard_map(
        functools.partial(local, mesh.shape["dp"], mesh.shape["tile"]),
        mesh=mesh,
        in_specs=(split, P("dp", "tile", None), P(), P(), P(), P(), split),
        out_specs=(split, split, P(), P(), P(), P()),
        check_vma=False,
    )
```

```python
import functools

import jax
import jax.numpy as jnp
from jax import lax
from jax.experimental import pallas as pl
from jax.experimental.pallas import tpu as pltpu
from jax.sharding import PartitionSpec as P

BLK = 8
LANES = 128
EPSILON = 1e-05
MESH = pl.DeviceIdType.MESH
F32 = jnp.float32
BF16 = jnp.bfloat16


def kernel(
    n_dp, n_tile, ch, nx, hy,
    x_hbm, d_hbm, occ_hbm, k1_hbm, k2_hbm, gain_hbm, shift_hbm,
    so_ref, ig_ref, q4, sums_out,
    occ_ref, k1_ref, k2_ref, gain_ref, shift_ref, raw, tall, in_sem,
    w1_ref, w2_ref, w1f_ref, w2f_ref, xd_pad, a_pad, i_pad, s_x, s_d, s_t, d3, ar, part, rp, half, r1,
    halo_s, halo_r, ar_s, ar_r, rs_s, rs_r,
):
    n_z = n_tile // 2
    n_chips, n_all = n_dp * n_z, n_dp * n_tile
    dp, tile = lax.axis_index("dp"), lax.axis_index("tile")
    core, z = lax.rem(tile, 2), tile // 2
    me, chip = dp * n_tile + tile, dp * n_z + z
    flat = nx * hy
    rows_half = half.shape[1]
    size = r1.shape[2]
    owners = rows_half // size

    def each(count, body):
        def step(k, carry):
            body(k)
            return carry
        lax.fori_loop(1, count, step, 0, unroll=count <= 32)

    def peer(k):
        other = lax.rem(me + k, n_all)
        return (other // n_tile, lax.rem(other, n_tile))

    def chip_peer(k):
        other = lax.rem(chip + k, n_chips)
        return other, (other // n_z, lax.rem(other, n_z) * 2 + core)

    sibling = (dp, z * 2 + 1 - core)
    has_left, has_right = tile > 0, tile < n_tile - 1

    barrier = pltpu.get_barrier_semaphore()
    each(n_all, lambda k: pl.semaphore_signal(
        barrier, inc=1, device_id=peer(k), device_id_type=MESH))

    loads = [pltpu.make_async_copy(src, dst, in_sem.at[i]) for i, (src, dst) in enumerate((
        (occ_hbm, occ_ref), (x_hbm, raw.at[0]), (d_hbm, raw.at[1]), (k1_hbm, k1_ref),
        (k2_hbm, k2_ref), (gain_hbm, gain_ref), (shift_hbm, shift_ref)))]
    for load in loads:
        load.start()

    width = hy // BLK
    spot = lax.broadcasted_iota(jnp.int32, (1, flat), 1)
    block_x, block_y = spot // (hy * BLK), lax.rem(spot, width) // BLK
    mask = jnp.zeros((1, flat), F32)
    loads[0].wait()
    for bx in range(nx // BLK):
        for by in range(width // BLK):
            mask = jnp.where((block_x == bx) & (block_y == by),
                             occ_ref[bx, by].astype(F32), mask)
    for i in range(2):
        loads[1 + i].wait()
        tall[i] = raw[i].astype(F32).reshape(ch * nx, hy)
        for x in range(nx):
            xd_pad[pl.ds(i * ch, ch), pl.ds((x + 1) * hy, hy)] = (
                tall[i, pl.ds(x, ch, stride=nx), :] * mask[:, x * hy:(x + 1) * hy]).astype(BF16)
    for load in loads[3:]:
        load.wait()
    same = (lax.broadcasted_iota(jnp.int32, (ch, ch), 0)
            == lax.broadcasted_iota(jnp.int32, (ch, ch), 1)).astype(BF16)

    def as_matrix(taps, out):
        for a in range(3):
            out[pl.ds(a * ch, ch), :] = lax.dot_general(
                same, taps[pl.ds(a * 9 * ch, 9 * ch), :], (((1,), (1,)), ((), ())),
                preferred_element_type=F32).astype(BF16)

    def as_flipped(taps, out):
        for a in range(3):
            out[pl.ds(a * ch, ch), :] = jnp.concatenate(
                [taps[pl.ds((26 - 9 * a - k) * ch, ch), :] for k in range(9)], axis=1)

    as_matrix(k1_ref, w1_ref)

    pl.semaphore_wait(barrier, n_all - 1)

    def halo(phase, src, first, pad):
        low = pltpu.make_async_remote_copy(
            src_ref=src.at[:, pl.ds(first, hy)],
            dst_ref=pad.at[:, pl.ds(flat + hy, hy)],
            send_sem=halo_s.at[phase, 0], recv_sem=halo_r.at[phase, 0],
            device_id=(dp, tile - 1), device_id_type=MESH)
        high = pltpu.make_async_remote_copy(
            src_ref=src.at[:, pl.ds(first + flat - hy, hy)],
            dst_ref=pad.at[:, pl.ds(0, hy)],
            send_sem=halo_s.at[phase, 1], recv_sem=halo_r.at[phase, 1],
            device_id=(dp, tile + 1), device_id_type=MESH)

        @pl.when(has_left)
        def _():
            low.start()

        @pl.when(has_right)
        def _():
            high.start()

        def finish():
            @pl.when(has_left)
            def _():
                low.wait_send()
                high.wait_recv()

            @pl.when(has_right)
            def _():
                high.wait_send()
                low.wait_recv()

        return finish

    def zero_ends(pad):
        @pl.when(jnp.logical_not(has_left))
        def _():
            pad[:, pl.ds(0, hy)] = jnp.zeros((pad.shape[0], hy), pad.dtype)

        @pl.when(jnp.logical_not(has_right))
        def _():
            pad[:, pl.ds(flat + hy, hy)] = jnp.zeros((pad.shape[0], hy), pad.dtype)

    lane = lax.broadcasted_iota(jnp.int32, (1, hy), 1)
    row_h, row_y = lane // width, lax.rem(lane, width)

    def shifts(pad, first, out, inner=True, outer=True):
        def plane(x, carry):
            at = pl.ds(x * hy if isinstance(x, int) else pl.multiple_of(x * hy, hy), hy)
            values = pad[pl.ds(first, ch), at]
            for b in range(3):
                for c in range(3):
                    step = (b - 1) * width + (c - 1)
                    moved = values
                    if step:
                        moved = pltpu.roll(values, (-step) % hy, 1)
                        fits = ((row_h + (b - 1) >= 0) & (row_h + (b - 1) < BLK)
                                & (row_y + (c - 1) >= 0) & (row_y + (c - 1) < width))
                        moved = jnp.where(fits, moved, jnp.zeros_like(moved))
                    out[pl.ds((3 * b + c) * ch, ch), at] = moved.astype(BF16)
            return carry
        if inner:
            lax.fori_loop(1, nx + 1, plane, 0, unroll=True)
        if outer:
            plane(0, 0)
            plane(nx + 1, 0)

    def conv(weight, stack):
        grown = jnp.dot(weight[...], stack[...], preferred_element_type=F32)
        return (grown[:ch, :flat] + grown[ch:2 * ch, hy:hy + flat]
                + grown[2 * ch:, 2 * hy:2 * hy + flat])

    nt = (((1,), (1,)), ((), ()))
    used = 27 * ch // 2

    def grad_by_input(stack, g):
        rows = 9 * ch
        side = rows // 2
        part[g, pl.ds(0, rows), :] = lax.dot_general(
            stack[...], d3[pl.ds(0, 2 * ch), :], nt, preferred_element_type=F32)
        rest = lax.dot_general(
            stack[...], d3[pl.ds(2 * ch, ch), :], nt, preferred_element_type=F32)
        part[g, pl.ds(rows, side), :] = jnp.concatenate([rest[:side], rest[side:]], axis=1)

    def grad_by_output(stack, g):
        rows = 3 * ch
        side = rows // 2
        for m in range(4):
            part[g, pl.ds(m * rows, rows), :] = lax.dot_general(
                d3[...], stack[pl.ds(m * 2 * ch, 2 * ch), :], nt, preferred_element_type=F32)
        rest = lax.dot_general(
            d3[...], stack[pl.ds(8 * ch, ch), :], nt, preferred_element_type=F32)
        part[g, pl.ds(4 * rows, side), :] = jnp.concatenate([rest[:side], rest[side:]], axis=1)

    def put_d3(value):
        for a in range(3):
            d3[pl.ds(a * ch, ch), pl.ds(a * hy, flat)] = value

    def to_rows(columns):
        spot = lax.broadcasted_iota(jnp.int32, (ch, LANES), 1)
        block = jnp.zeros((ch, LANES), F32)
        for index, column in enumerate(columns):
            block = jnp.where(spot == index, column, block)
        return jnp.transpose(block)[:8]

    def to_columns(rows):
        return jnp.transpose(jnp.concatenate([rows, jnp.zeros((LANES - 8, ch), F32)], axis=0))

    def small_start(call, first, second, third):
        ar[call, me, 0:1, :] = jnp.concatenate([first, second], axis=1)
        ar[call, me, 1:2, :] = jnp.concatenate([third, third], axis=1)
        each(n_all, lambda k: pltpu.make_async_remote_copy(
            src_ref=ar.at[call, me], dst_ref=ar.at[call, me],
            send_sem=ar_s.at[call], recv_sem=ar_r.at[call],
            device_id=peer(k), device_id_type=MESH).start())

    def small_end(call):
        arrived = ar.at[call, pl.ds(0, n_all - 1)]
        pltpu.make_async_copy(arrived, arrived, ar_r.at[call]).wait()
        pltpu.make_async_copy(arrived, arrived, ar_s.at[call]).wait()
        return ar[call, :, 0, :], ar[call, :, 1, :]

    def merge_moments(sums_squares, counts):
        total = jnp.sum(sums_squares, axis=0, keepdims=True)
        count = jnp.sum(counts, axis=0, keepdims=True)
        off = (sums_squares / jnp.maximum(counts, 1.0) - total / jnp.maximum(count, 1.0))
        between = jnp.sum(counts * off * off, axis=0, keepdims=True)
        return jnp.concatenate(
            [total[:, :ch], total[:, ch:] + between[:, :ch], count[:, :ch],
             jnp.zeros((5, ch), F32)], axis=0)

    def scatter_core(g):
        theirs = pl.ds(pl.multiple_of((1 - core) * rows_half, rows_half), rows_half)
        copy = pltpu.make_async_remote_copy(
            src_ref=part.at[g, theirs, :], dst_ref=rp.at[g],
            send_sem=rs_s.at[g, 0], recv_sem=rs_r.at[g, 0],
            device_id=sibling, device_id_type=MESH)
        copy.start()
        return copy

    def settle(g, stage, ref):
        pltpu.make_async_copy(ref, ref, rs_r.at[g, stage]).wait()

    def drain(g, stage, ref):
        pltpu.make_async_copy(ref, ref, rs_s.at[g, stage]).wait()

    def scatter_chips(g, copy):
        copy.wait()
        mine = pl.ds(pl.multiple_of(core * rows_half, rows_half), rows_half)
        total = part[g, mine, :] + rp[g]
        rp[g] = total
        half[g] = total.astype(BF16)

        def send(k):
            other, device = chip_peer(k)

            @pl.when(other < owners)
            def _():
                pltpu.make_async_remote_copy(
                    src_ref=half.at[g, pl.ds(pl.multiple_of(other * size, size), size), :],
                    dst_ref=r1.at[g, k - 1],
                    send_sem=rs_s.at[g, 1], recv_sem=rs_r.at[g, 1],
                    device_id=device, device_id_type=MESH).start()

        each(n_chips, send)

    def gather_chips(g):
        @pl.when(chip < owners)
        def _():
            settle(g, 1, r1.at[g])
            total = rp[g, pl.ds(pl.multiple_of(chip * size, size), size), :]
            for k in range(n_chips - 1):
                total = total + r1[g, k].astype(F32)
            place = pl.ds(pl.multiple_of(core * rows_half + chip * size, size), size)
            q4[g, place, :] = total.astype(BF16)

            def send(k):
                _, device = chip_peer(k)
                pltpu.make_async_remote_copy(
                    src_ref=q4.at[g, place, :], dst_ref=q4.at[g, place, :],
                    send_sem=rs_s.at[g, 2], recv_sem=rs_r.at[g, 2],
                    device_id=device, device_id_type=MESH).start()

            each(n_chips, send)

    def gather_core(g):
        @pl.when(chip < owners)
        def _():
            settle(g, 2, half.at[g, pl.ds(0, (owners - 1) * size), :])
            drain(g, 1, half.at[g, pl.ds(0, (owners - 1) * size), :])
            drain(g, 2, r1.at[g])

        @pl.when(chip >= owners)
        def _():
            settle(g, 2, half.at[g])
            drain(g, 1, half.at[g])

        mine = pl.ds(pl.multiple_of(core * rows_half, rows_half), rows_half)
        copy = pltpu.make_async_remote_copy(
            src_ref=q4.at[g, mine, :], dst_ref=q4.at[g, mine, :],
            send_sem=rs_s.at[g, 3], recv_sem=rs_r.at[g, 3],
            device_id=sibling, device_id_type=MESH)
        copy.start()
        return copy

    end_xd = halo(0, xd_pad, hy, xd_pad)
    shifts(xd_pad, 0, s_x, outer=False)
    zero_ends(xd_pad)
    zero_ends(a_pad)
    zero_ends(i_pad)
    end_xd()

    shifts(xd_pad, 0, s_x, inner=False)
    pre = conv(w1_ref, s_x)
    count_here = jnp.sum(mask, axis=1, keepdims=True)
    sums_here = jnp.sum(pre * mask, axis=1, keepdims=True)
    off = (pre - sums_here / jnp.maximum(count_here, 1.0)) * mask
    squares_here = jnp.sum(off * off, axis=1, keepdims=True)
    rows = to_rows([sums_here, squares_here])
    small_start(0, rows[0:1], rows[1:2], jnp.broadcast_to(count_here, (1, ch)))

    shifts(xd_pad, ch, s_d)
    as_flipped(k2_ref, w2f_ref)
    act_grad = conv(w2f_ref, s_d)
    gain_shift = to_columns(jnp.concatenate(
        [gain_ref[...], shift_ref[...], jnp.zeros((6, ch), F32)], axis=0))
    d3[...] = jnp.zeros(d3.shape, d3.dtype)
    if part.shape[1] > used:
        for g in range(2):
            part[g, pl.ds(used, part.shape[1] - used), :] = jnp.zeros(
                (part.shape[1] - used, LANES), F32)
    as_matrix(k2_ref, w2_ref)
    as_flipped(k1_ref, w1f_ref)

    moments = to_columns(merge_moments(*small_end(0)))
    count = moments[:, 2:3]
    mean = moments[:, 0:1] / count
    inv_std = lax.rsqrt(moments[:, 1:2] / count + EPSILON)
    gain, shift = gain_shift[:, 0:1], gain_shift[:, 1:2]
    normal = (pre - mean) * inv_std
    pre_act = gain * normal + shift
    sg = 1.0 / (1.0 + jnp.exp(-pre_act))
    z_grad = act_grad * mask * sg * (1.0 + pre_act * (1.0 - sg))
    shift_here = jnp.sum(z_grad, axis=1, keepdims=True)
    gain_here = jnp.sum(z_grad * normal, axis=1, keepdims=True)
    rows = to_rows([shift_here, gain_here])
    small_start(1, rows[0:1], rows[1:2], rows[0:1])

    act = (pre_act * sg * mask).astype(BF16)
    a_pad[:, pl.ds(hy, flat)] = act
    end_act = halo(1, a_pad, hy, a_pad)
    put_d3(act)
    grad_by_output(s_d, 0)
    two = scatter_core(0)
    shifts(a_pad, 0, s_t, outer=False)
    scatter_chips(0, two)
    end_act()
    shifts(a_pad, 0, s_t, inner=False)
    pre_two = conv(w2_ref, s_t)
    so_ref[...] = ((xd_pad[pl.ds(0, ch), pl.ds(hy, flat)].astype(F32) + pre_two) * mask).astype(BF16)

    totals = jnp.sum(small_end(1)[0], axis=0, keepdims=True)
    totals = jnp.concatenate([totals[:, :ch], totals[:, ch:], jnp.zeros((6, ch), F32)], axis=0)
    sums_out[...] = totals
    totals = to_columns(totals)
    delta_one = (gain * inv_std * (
        z_grad - totals[:, 0:1] / count - normal * (totals[:, 1:2] / count)) * mask).astype(BF16)
    i_pad[:, pl.ds(hy, flat)] = delta_one
    end_delta = halo(2, i_pad, hy, i_pad)
    put_d3(delta_one)
    grad_by_input(s_x, 1)
    one = scatter_core(1)
    gather_chips(0)
    scatter_chips(1, one)
    shifts(i_pad, 0, s_t, outer=False)
    end_delta()
    shifts(i_pad, 0, s_t, inner=False)
    back = conv(w1f_ref, s_t)
    ig_ref[...] = ((xd_pad[pl.ds(ch, ch), pl.ds(hy, flat)].astype(F32) + back) * mask).astype(BF16)
    two = gather_core(0)
    gather_chips(1)
    one = gather_core(1)
    two.wait()
    one.wait()


def unpack(ch, so_in, ig_in, q4, sums, so_ref, ig_ref, g1_ref, g2_ref, gain_ref, shift_ref):
    rows = 9 * ch
    half = rows // 2
    for a in range(2):
        g1_ref[pl.ds(a * rows, rows), :] = q4[1, pl.ds(0, rows), pl.ds(a * ch, ch)].astype(F32)
    for side in range(2):
        g1_ref[pl.ds(2 * rows + side * half, half), :] = (
            q4[1, pl.ds(rows, half), pl.ds(side * ch, ch)].astype(F32))
    rows = 3 * ch
    half = rows // 2
    for a in range(3):
        for m in range(4):
            for side in range(2):
                g2_ref[pl.ds((26 - 9 * a - 2 * m - side) * ch, ch), :] = (
                    q4[0, pl.ds(m * rows + a * ch, ch), pl.ds(side * ch, ch)].astype(F32))
    step = ch // 2
    for part in range(6):
        side, row = part // 3, part % 3
        a, top = part // 2, part % 2
        g2_ref[pl.ds((18 - 9 * a) * ch + top * step, step), :] = (
            q4[0, pl.ds(4 * rows + row * step, step), pl.ds(side * ch, ch)].astype(F32))
    so_ref[...] = so_in[...]
    ig_ref[...] = ig_in[...]
    shift_ref[...] = sums[0:1, :]
    gain_ref[...] = sums[1:2, :]


def local(n_dp, n_tile, features, occupied, conv_one, conv_two, gain, shift, cotangent):
    scenes, ch, nx, hy = features.shape
    flat = nx * hy
    n_chips, n_all = n_dp * n_tile // 2, n_dp * n_tile
    used = 27 * ch // 2
    size = -(-used // (2 * n_chips * 16)) * 16
    rows_half = -(-used // (2 * size)) * size
    rows = 2 * rows_half
    vmem = pl.BlockSpec(memory_space=pltpu.VMEM)
    dma = pltpu.SemaphoreType.DMA
    so, ig, q4, sums = pl.pallas_call(
        functools.partial(kernel, n_dp, n_tile, ch, nx, hy),
        out_shape=(
            jax.ShapeDtypeStruct((ch, flat), BF16),
            jax.ShapeDtypeStruct((ch, flat), BF16),
            jax.ShapeDtypeStruct((2, rows, LANES), BF16),
            jax.ShapeDtypeStruct((8, ch), F32),
        ),
        in_specs=[pl.BlockSpec(memory_space=pltpu.HBM)] * 7,
        out_specs=[vmem] * 4,
        scratch_shapes=[
            pltpu.SMEM(occupied.shape[1:], jnp.int32),
            pltpu.VMEM((27 * ch, ch), BF16),
            pltpu.VMEM((27 * ch, ch), BF16),
            pltpu.VMEM((1, ch), F32),
            pltpu.VMEM((1, ch), F32),
            pltpu.VMEM((2, ch, nx, hy), BF16),
            pltpu.VMEM((2, ch * nx, hy), F32),
            dma((7,)),
            pltpu.VMEM((3 * ch, 9 * ch), BF16),
            pltpu.VMEM((3 * ch, 9 * ch), BF16),
            pltpu.VMEM((3 * ch, 9 * ch), BF16),
            pltpu.VMEM((3 * ch, 9 * ch), BF16),
            pltpu.VMEM((2 * ch, flat + 2 * hy), BF16),
            pltpu.VMEM((ch, flat + 2 * hy), BF16),
            pltpu.VMEM((ch, flat + 2 * hy), BF16),
            pltpu.VMEM((9 * ch, flat + 2 * hy), BF16),
            pltpu.VMEM((9 * ch, flat + 2 * hy), BF16),
            pltpu.VMEM((9 * ch, flat + 2 * hy), BF16),
            pltpu.VMEM((3 * ch, flat + 2 * hy), BF16),
            pltpu.VMEM((2, n_all, 2, LANES), F32),
            pltpu.VMEM((2, rows, LANES), F32),
            pltpu.VMEM((2, rows_half, LANES), F32),
            pltpu.VMEM((2, rows_half, LANES), BF16),
            pltpu.VMEM((2, n_chips - 1, size, LANES), BF16),
            dma((3, 2)), dma((3, 2)),
            dma((2,)), dma((2,)),
            dma((2, 4)), dma((2, 4)),
        ],
        compiler_params=pltpu.CompilerParams(
            collective_id=0, has_side_effects=True, vmem_limit_bytes=48 * 2**20),
    )(
        *(pltpu.with_memory_space_constraint(value, pltpu.HBM) for value in (
            features[0], cotangent[0], occupied[0], conv_one.reshape(27 * ch, ch),
            conv_two.reshape(27 * ch, ch), gain.reshape(1, ch), shift.reshape(1, ch))))
    planes = features.shape[1:]
    so, ig, g1, g2, gg, sg = pl.pallas_call(
        functools.partial(unpack, ch),
        out_shape=(
            jax.ShapeDtypeStruct(planes, BF16),
            jax.ShapeDtypeStruct(planes, BF16),
            jax.ShapeDtypeStruct((27 * ch, ch), F32),
            jax.ShapeDtypeStruct((27 * ch, ch), F32),
            jax.ShapeDtypeStruct((1, ch), F32),
            jax.ShapeDtypeStruct((1, ch), F32),
        ),
        in_specs=[vmem] * 4,
        out_specs=[vmem] * 6,
        compiler_params=pltpu.CompilerParams(vmem_limit_bytes=16 * 2**20),
    )(so.reshape(planes), ig.reshape(planes), q4, sums)
    shape = features.shape
    return (so.reshape(shape), ig.reshape(shape), g1.reshape(27, ch, ch),
            g2.reshape(27, ch, ch), gg.reshape(ch), sg.reshape(ch))


def solution(mesh):
    split = P("dp", None, "tile", None)
    return jax.shard_map(
        functools.partial(local, mesh.shape["dp"], mesh.shape["tile"]),
        mesh=mesh,
        in_specs=(split, P("dp", "tile", None), P(), P(), P(), P(), split),
        out_specs=(split, split, P(), P(), P(), P()),
        check_vma=False,
    )
```

```python
import functools

import jax
import jax.numpy as jnp
from jax import lax
from jax.experimental import pallas as pl
from jax.experimental.pallas import tpu as pltpu
from jax.sharding import PartitionSpec as P

BLK = 8
LANES = 128
EPSILON = 1e-05
MESH = pl.DeviceIdType.MESH
F32 = jnp.float32
BF16 = jnp.bfloat16


def kernel(
    n_dp, n_tile, ch, nx, hy,
    x_hbm, d_hbm, occ_hbm, k1_hbm, k2_hbm, gain_hbm, shift_hbm,
    so_ref, ig_ref, q4, sums_out,
    occ_ref, k1_ref, k2_ref, gain_ref, shift_ref, raw, tall, in_sem,
    w1_ref, w2_ref, w1f_ref, w2f_ref, xd_pad, a_pad, i_pad, s_x, s_d, s_t, d3, ar, part, rp, half, r1,
    halo_s, halo_r, ar_s, ar_r, rs_s, rs_r,
):
    n_z = n_tile // 2
    n_chips, n_all = n_dp * n_z, n_dp * n_tile
    dp, tile = lax.axis_index("dp"), lax.axis_index("tile")
    core, z = lax.rem(tile, 2), tile // 2
    me, chip = dp * n_tile + tile, dp * n_z + z
    flat = nx * hy
    size = r1.shape[2]
    group = n_z * size
    used = 27 * ch // 2
    blocks = -(-used // size)
    rows_core = (n_chips * size, -(-used // (2 * size)) * size)
    owners = ((min(blocks, n_chips), blocks - min(blocks, n_chips)), (rows_core[1] // size,) * 2)

    def each(count, body):
        def step(k, carry):
            body(k)
            return carry
        lax.fori_loop(1, count, step, 0, unroll=count <= 32)

    def peer(k):
        other = lax.rem(me + k, n_all)
        return (other // n_tile, lax.rem(other, n_tile))

    def chip_peer(k):
        other = lax.rem(chip + k, n_chips)
        return other, (other // n_z, lax.rem(other, n_z) * 2 + core)

    sibling = (dp, z * 2 + 1 - core)
    has_left, has_right = tile > 0, tile < n_tile - 1

    barrier = pltpu.get_barrier_semaphore()
    each(n_all, lambda k: pl.semaphore_signal(
        barrier, inc=1, device_id=peer(k), device_id_type=MESH))

    loads = [pltpu.make_async_copy(src, dst, in_sem.at[i]) for i, (src, dst) in enumerate((
        (occ_hbm, occ_ref), (x_hbm, raw.at[0]), (d_hbm, raw.at[1]), (k1_hbm, k1_ref),
        (k2_hbm, k2_ref), (gain_hbm, gain_ref), (shift_hbm, shift_ref)))]
    for load in loads:
        load.start()

    width = hy // BLK
    spot = lax.broadcasted_iota(jnp.int32, (1, flat), 1)
    block_x, block_y = spot // (hy * BLK), lax.rem(spot, width) // BLK
    mask = jnp.zeros((1, flat), F32)
    loads[0].wait()
    for bx in range(nx // BLK):
        for by in range(width // BLK):
            mask = jnp.where((block_x == bx) & (block_y == by),
                             occ_ref[bx, by].astype(F32), mask)
    for i in range(2):
        loads[1 + i].wait()
        tall[i] = raw[i].astype(F32).reshape(ch * nx, hy)
        for x in range(nx):
            xd_pad[pl.ds(i * ch, ch), pl.ds((x + 1) * hy, hy)] = (
                tall[i, pl.ds(x, ch, stride=nx), :] * mask[:, x * hy:(x + 1) * hy]).astype(BF16)
    for load in loads[3:]:
        load.wait()
    same = (lax.broadcasted_iota(jnp.int32, (ch, ch), 0)
            == lax.broadcasted_iota(jnp.int32, (ch, ch), 1)).astype(BF16)

    def as_matrix(taps, out):
        for a in range(3):
            out[pl.ds(a * ch, ch), :] = lax.dot_general(
                same, taps[pl.ds(a * 9 * ch, 9 * ch), :], (((1,), (1,)), ((), ())),
                preferred_element_type=F32).astype(BF16)

    def as_flipped(taps, out):
        for a in range(3):
            out[pl.ds(a * ch, ch), :] = jnp.concatenate(
                [taps[pl.ds((26 - 9 * a - k) * ch, ch), :] for k in range(9)], axis=1)

    as_matrix(k1_ref, w1_ref)

    pl.semaphore_wait(barrier, n_all - 1)

    def halo(phase, src, first, pad):
        low = pltpu.make_async_remote_copy(
            src_ref=src.at[:, pl.ds(first, hy)],
            dst_ref=pad.at[:, pl.ds(flat + hy, hy)],
            send_sem=halo_s.at[phase, 0], recv_sem=halo_r.at[phase, 0],
            device_id=(dp, tile - 1), device_id_type=MESH)
        high = pltpu.make_async_remote_copy(
            src_ref=src.at[:, pl.ds(first + flat - hy, hy)],
            dst_ref=pad.at[:, pl.ds(0, hy)],
            send_sem=halo_s.at[phase, 1], recv_sem=halo_r.at[phase, 1],
            device_id=(dp, tile + 1), device_id_type=MESH)

        @pl.when(has_left)
        def _():
            low.start()

        @pl.when(has_right)
        def _():
            high.start()

        def finish():
            @pl.when(has_left)
            def _():
                low.wait_send()
                high.wait_recv()

            @pl.when(has_right)
            def _():
                high.wait_send()
                low.wait_recv()

        return finish

    def zero_ends(pad):
        @pl.when(jnp.logical_not(has_left))
        def _():
            pad[:, pl.ds(0, hy)] = jnp.zeros((pad.shape[0], hy), pad.dtype)

        @pl.when(jnp.logical_not(has_right))
        def _():
            pad[:, pl.ds(flat + hy, hy)] = jnp.zeros((pad.shape[0], hy), pad.dtype)

    lane = lax.broadcasted_iota(jnp.int32, (1, hy), 1)
    row_h, row_y = lane // width, lax.rem(lane, width)

    def shifts(pad, first, out, inner=True, outer=True):
        def plane(x, carry):
            at = pl.ds(x * hy if isinstance(x, int) else pl.multiple_of(x * hy, hy), hy)
            values = pad[pl.ds(first, ch), at]
            for b in range(3):
                for c in range(3):
                    step = (b - 1) * width + (c - 1)
                    moved = values
                    if step:
                        moved = pltpu.roll(values, (-step) % hy, 1)
                        fits = ((row_h + (b - 1) >= 0) & (row_h + (b - 1) < BLK)
                                & (row_y + (c - 1) >= 0) & (row_y + (c - 1) < width))
                        moved = jnp.where(fits, moved, jnp.zeros_like(moved))
                    out[pl.ds((3 * b + c) * ch, ch), at] = moved.astype(BF16)
            return carry
        if inner:
            lax.fori_loop(1, nx + 1, plane, 0, unroll=True)
        if outer:
            plane(0, 0)
            plane(nx + 1, 0)

    def conv(weight, stack):
        grown = jnp.dot(weight[...], stack[...], preferred_element_type=F32)
        return (grown[:ch, :flat] + grown[ch:2 * ch, hy:hy + flat]
                + grown[2 * ch:, 2 * hy:2 * hy + flat])

    nt = (((1,), (1,)), ((), ()))

    def grad_by_input(stack, g, which):
        count = 9 * ch // 2
        side = count // 2
        first = which * rows_core[g]
        found = lax.dot_general(
            stack[span(which * count, count, 16), :], d3[...], nt, preferred_element_type=F32)
        part[g, span(first, count, 8), :] = found[:, :2 * ch]
        part[g, span(first + count, side, 8), :] = jnp.concatenate(
            [found[:side, 2 * ch:], found[side:, 2 * ch:]], axis=1)

    def grad_by_output(stack, g):
        rows = 3 * ch
        side = rows // 2
        found = lax.dot_general(d3[...], stack[...], nt, preferred_element_type=F32)
        for m in range(4):
            part[g, pl.ds(m * rows, rows), :] = found[:, m * 2 * ch:(m + 1) * 2 * ch]
        part[g, pl.ds(4 * rows, side), :] = jnp.concatenate(
            [found[:side, 8 * ch:], found[side:, 8 * ch:]], axis=1)

    def span(start, count, step):
        return pl.ds(pl.multiple_of(start, step), count)

    def put_d3(value):
        for a in range(3):
            d3[pl.ds(a * ch, ch), pl.ds(a * hy, flat)] = value

    def to_rows(columns):
        spot = lax.broadcasted_iota(jnp.int32, (ch, LANES), 1)
        block = jnp.zeros((ch, LANES), F32)
        for index, column in enumerate(columns):
            block = jnp.where(spot == index, column, block)
        return jnp.transpose(block)[:8]

    def to_columns(rows):
        return jnp.transpose(jnp.concatenate([rows, jnp.zeros((LANES - 8, ch), F32)], axis=0))

    def small_start(call, first, second, third):
        ar[call, me, 0:1, :] = jnp.concatenate([first, second], axis=1)
        ar[call, me, 1:2, :] = jnp.concatenate([third, third], axis=1)
        each(n_all, lambda k: pltpu.make_async_remote_copy(
            src_ref=ar.at[call, me], dst_ref=ar.at[call, me],
            send_sem=ar_s.at[call], recv_sem=ar_r.at[call],
            device_id=peer(k), device_id_type=MESH).start())

    def small_end(call):
        arrived = ar.at[call, pl.ds(0, n_all - 1)]
        pltpu.make_async_copy(arrived, arrived, ar_r.at[call]).wait()
        pltpu.make_async_copy(arrived, arrived, ar_s.at[call]).wait()
        return ar[call, :, 0, :], ar[call, :, 1, :]

    def merge_moments(sums_squares, counts):
        total = jnp.sum(sums_squares, axis=0, keepdims=True)
        count = jnp.sum(counts, axis=0, keepdims=True)
        off = (sums_squares / jnp.maximum(counts, 1.0) - total / jnp.maximum(count, 1.0))
        between = jnp.sum(counts * off * off, axis=0, keepdims=True)
        return jnp.concatenate(
            [total[:, :ch], total[:, ch:] + between[:, :ch], count[:, :ch],
             jnp.zeros((5, ch), F32)], axis=0)

    def by_core(g, body):
        for side in range(2):
            count = owners[g][side]
            pl.when((core == side) & (chip < count))(lambda: body(True, count))
            pl.when((core == side) & (chip >= count))(lambda: body(False, count))

    def settle(g, stage, ref):
        pltpu.make_async_copy(ref, ref, rs_r.at[g, stage]).wait()

    def drain(g, stage, ref):
        pltpu.make_async_copy(ref, ref, rs_s.at[g, stage]).wait()

    def send(g, stage, src, dst, device):
        pltpu.make_async_remote_copy(
            src_ref=src, dst_ref=dst, send_sem=rs_s.at[g, stage], recv_sem=rs_r.at[g, stage],
            device_id=device, device_id_type=MESH).start()

    def scatter_core(g):
        rows = rows_core[g]
        send(g, 0, part.at[g, span((1 - core) * rows, rows, size), :], rp.at[g, pl.ds(0, rows), :],
             sibling)

    def add_core(g):
        rows = rows_core[g]
        done = rp.at[g, pl.ds(0, rows), :]
        settle(g, 0, done)
        drain(g, 0, done)
        total = part[g, span(core * rows, rows, size), :] + rp[g, pl.ds(0, rows), :]
        rp[g, pl.ds(0, rows), :] = total
        return total

    def scatter_chips(g):
        half[g, pl.ds(0, rows_core[g]), :] = add_core(g).astype(BF16)
        here = jnp.where(core == 0, owners[g][0], owners[g][1])

        def step(k):
            other, device = chip_peer(k)

            @pl.when(other < here)
            def _():
                send(g, 1, half.at[g, span(other * size, size, size), :], r1.at[g, k - 1], device)

        each(n_chips, step)

    def sum_chips(g, owned):
        place = q4.at[g, span(core * rows_core[g] + chip * size, size, size), :]
        if owned:
            settle(g, 1, r1.at[g])
            total = rp[g, span(chip * size, size, size), :]
            for k in range(n_chips - 1):
                total = total + r1[g, k].astype(F32)
            place[...] = total.astype(BF16)
        else:
            place[...] = jnp.zeros((size, LANES), BF16)
        return place

    def drain_chips(g, owned, count):
        if count > owned:
            drain(g, 1, half.at[g, pl.ds(0, (count - owned) * size), :])

    def gather_chips(g):
        def body(owned, count):
            if owned:
                place = sum_chips(g, owned)
                each(n_chips, lambda k: send(g, 2, place, place, chip_peer(k)[1]))
        by_core(g, body)

    def gather_core(g):
        rows = rows_core[g]
        mine = q4.at[g, span(core * rows, rows, size), :]
        send(g, 3, mine, mine, sibling)

    def end_core(g):
        rows = q4.at[g, pl.ds(0, rows_core[g]), :]
        settle(g, 3, rows)
        drain(g, 3, rows)

    def end_chips(g):
        def body(owned, count):
            drain_chips(g, owned, count)
            settle(g, 2, half.at[g, pl.ds(0, (count - owned) * size), :])
            if owned:
                drain(g, 2, r1.at[g])
        by_core(g, body)

    def plane_peer(k):
        other = lax.rem(dp + k, n_dp)
        return other, (other, tile)

    def line_peer(k):
        other = lax.rem(z + k, n_z)
        return other, (dp, other * 2 + core)

    def gather_line(g):
        def body(owned, count):
            sum_chips(g, owned)
            drain_chips(g, owned, count)
        by_core(g, body)
        place = q4.at[g, span(core * rows_core[g] + chip * size, size, size), :]
        each(n_z, lambda k: send(g, 4, place, place, line_peer(k)[1]))

    def gather_plane(g):
        others = q4.at[g, pl.ds(0, (n_z - 1) * size), :]
        settle(g, 4, others)
        place = q4.at[g, span(core * rows_core[g] + dp * group, group, size), :]
        each(n_dp, lambda k: send(g, 5, place, place, plane_peer(k)[1]))
        drain(g, 4, others)

    def end_plane(g):
        others = q4.at[g, pl.ds(0, (n_dp - 1) * group), :]
        settle(g, 5, others)
        drain(g, 5, others)

    end_xd = halo(0, xd_pad, hy, xd_pad)
    shifts(xd_pad, 0, s_x, outer=False)
    zero_ends(xd_pad)
    zero_ends(a_pad)
    zero_ends(i_pad)
    inside = jnp.dot(w1_ref[...], s_x[:, pl.ds(hy, flat)], preferred_element_type=F32)
    end_xd()

    shifts(xd_pad, 0, s_x, inner=False)
    before = jnp.dot(w1_ref[pl.ds(0, ch), :], s_x[:, pl.ds(0, hy)], preferred_element_type=F32)
    after = jnp.dot(w1_ref[pl.ds(2 * ch, ch), :], s_x[:, pl.ds(hy + flat, hy)],
                    preferred_element_type=F32)
    pre = (inside[ch:2 * ch]
           + jnp.concatenate([before, inside[:ch, :flat - hy]], axis=1)
           + jnp.concatenate([inside[2 * ch:, hy:], after], axis=1))
    count_here = jnp.sum(mask, axis=1, keepdims=True)
    sums_here = jnp.sum(pre * mask, axis=1, keepdims=True)
    off = (pre - sums_here / jnp.maximum(count_here, 1.0)) * mask
    squares_here = jnp.sum(off * off, axis=1, keepdims=True)
    rows = to_rows([sums_here, squares_here])
    small_start(0, rows[0:1], rows[1:2], jnp.broadcast_to(count_here, (1, ch)))

    shifts(xd_pad, ch, s_d)
    as_flipped(k2_ref, w2f_ref)
    act_grad = conv(w2f_ref, s_d)
    gain_shift = to_columns(jnp.concatenate(
        [gain_ref[...], shift_ref[...], jnp.zeros((6, ch), F32)], axis=0))
    d3[...] = jnp.zeros(d3.shape, d3.dtype)
    for g, (first, last) in ((0, (used, 2 * rows_core[0])),
                             (1, (used // 2, rows_core[1])),
                             (1, (rows_core[1] + used // 2, 2 * rows_core[1]))):
        if last > first:
            part[g, pl.ds(first, last - first), :] = jnp.zeros((last - first, LANES), F32)
    as_matrix(k2_ref, w2_ref)
    as_flipped(k1_ref, w1f_ref)

    moments = to_columns(merge_moments(*small_end(0)))
    count = moments[:, 2:3]
    mean = moments[:, 0:1] / count
    inv_std = lax.rsqrt(moments[:, 1:2] / count + EPSILON)
    gain, shift = gain_shift[:, 0:1], gain_shift[:, 1:2]
    normal = (pre - mean) * inv_std
    pre_act = gain * normal + shift
    sg = 1.0 / (1.0 + jnp.exp(-pre_act))
    z_grad = act_grad * mask * sg * (1.0 + pre_act * (1.0 - sg))
    shift_here = jnp.sum(z_grad, axis=1, keepdims=True)
    gain_here = jnp.sum(z_grad * normal, axis=1, keepdims=True)
    rows = to_rows([shift_here, gain_here])
    small_start(1, rows[0:1], rows[1:2], rows[0:1])

    act = (pre_act * sg * mask).astype(BF16)
    a_pad[:, pl.ds(hy, flat)] = act
    end_act = halo(1, a_pad, hy, a_pad)
    put_d3(act)
    grad_by_output(s_d, 0)
    scatter_core(0)
    shifts(a_pad, 0, s_t, outer=False)
    scatter_chips(0)
    end_act()
    shifts(a_pad, 0, s_t, inner=False)
    pre_two = conv(w2_ref, s_t)
    so_ref[...] = ((xd_pad[pl.ds(0, ch), pl.ds(hy, flat)].astype(F32) + pre_two) * mask).astype(BF16)

    totals = jnp.sum(small_end(1)[0], axis=0, keepdims=True)
    totals = jnp.concatenate([totals[:, :ch], totals[:, ch:], jnp.zeros((6, ch), F32)], axis=0)
    sums_out[...] = totals
    totals = to_columns(totals)
    delta_one = (gain * inv_std * (
        z_grad - totals[:, 0:1] / count - normal * (totals[:, 1:2] / count)) * mask).astype(BF16)
    i_pad[:, pl.ds(hy, flat)] = delta_one
    end_delta = halo(2, i_pad, hy, i_pad)
    put_d3(delta_one)
    grad_by_input(s_x, 1, 1 - core)
    scatter_core(1)
    grad_by_input(s_x, 1, core)
    gather_line(0)
    scatter_chips(1)
    shifts(i_pad, 0, s_t, outer=False)
    end_delta()
    shifts(i_pad, 0, s_t, inner=False)
    back = conv(w1f_ref, s_t)
    ig_ref[...] = ((xd_pad[pl.ds(ch, ch), pl.ds(hy, flat)].astype(F32) + back) * mask).astype(BF16)
    gather_plane(0)
    gather_chips(1)
    end_plane(0)
    gather_core(0)
    end_chips(1)
    gather_core(1)
    end_core(0)
    end_core(1)


def unpack(ch, rows_core, so_in, ig_in, q4, sums, so_ref, ig_ref, g1_ref, g2_ref, gain_ref, shift_ref):
    count = 9 * ch // 2
    side = count // 2
    for core in range(2):
        first = core * rows_core
        for a in range(2):
            g1_ref[pl.ds(a * 9 * ch + core * count, count), :] = (
                q4[1, pl.ds(first, count), pl.ds(a * ch, ch)].astype(F32))
        for k in range(2):
            g1_ref[pl.ds(18 * ch + core * count + k * side, side), :] = (
                q4[1, pl.ds(first + count, side), pl.ds(k * ch, ch)].astype(F32))
    rows = 3 * ch
    half = rows // 2
    for a in range(3):
        for m in range(4):
            for side in range(2):
                g2_ref[pl.ds((26 - 9 * a - 2 * m - side) * ch, ch), :] = (
                    q4[0, pl.ds(m * rows + a * ch, ch), pl.ds(side * ch, ch)].astype(F32))
    step = ch // 2
    for part in range(6):
        side, row = part // 3, part % 3
        a, top = part // 2, part % 2
        g2_ref[pl.ds((18 - 9 * a) * ch + top * step, step), :] = (
            q4[0, pl.ds(4 * rows + row * step, step), pl.ds(side * ch, ch)].astype(F32))
    so_ref[...] = so_in[...]
    ig_ref[...] = ig_in[...]
    shift_ref[...] = sums[0:1, :]
    gain_ref[...] = sums[1:2, :]


def local(n_dp, n_tile, features, occupied, conv_one, conv_two, gain, shift, cotangent):
    scenes, ch, nx, hy = features.shape
    flat = nx * hy
    n_chips, n_all = n_dp * n_tile // 2, n_dp * n_tile
    used = 27 * ch // 2
    size = -(-used // (2 * n_chips * 16)) * 16
    rows_half = -(-used // (2 * size)) * size
    rows = 2 * n_chips * size
    vmem = pl.BlockSpec(memory_space=pltpu.VMEM)
    dma = pltpu.SemaphoreType.DMA
    so, ig, q4, sums = pl.pallas_call(
        functools.partial(kernel, n_dp, n_tile, ch, nx, hy),
        out_shape=(
            jax.ShapeDtypeStruct((ch, flat), BF16),
            jax.ShapeDtypeStruct((ch, flat), BF16),
            jax.ShapeDtypeStruct((2, rows, LANES), BF16),
            jax.ShapeDtypeStruct((8, ch), F32),
        ),
        in_specs=[pl.BlockSpec(memory_space=pltpu.HBM)] * 7,
        out_specs=[vmem] * 4,
        scratch_shapes=[
            pltpu.SMEM(occupied.shape[1:], jnp.int32),
            pltpu.VMEM((27 * ch, ch), BF16),
            pltpu.VMEM((27 * ch, ch), BF16),
            pltpu.VMEM((1, ch), F32),
            pltpu.VMEM((1, ch), F32),
            pltpu.VMEM((2, ch, nx, hy), BF16),
            pltpu.VMEM((2, ch * nx, hy), F32),
            dma((7,)),
            pltpu.VMEM((3 * ch, 9 * ch), BF16),
            pltpu.VMEM((3 * ch, 9 * ch), BF16),
            pltpu.VMEM((3 * ch, 9 * ch), BF16),
            pltpu.VMEM((3 * ch, 9 * ch), BF16),
            pltpu.VMEM((2 * ch, flat + 2 * hy), BF16),
            pltpu.VMEM((ch, flat + 2 * hy), BF16),
            pltpu.VMEM((ch, flat + 2 * hy), BF16),
            pltpu.VMEM((9 * ch, flat + 2 * hy), BF16),
            pltpu.VMEM((9 * ch, flat + 2 * hy), BF16),
            pltpu.VMEM((9 * ch, flat + 2 * hy), BF16),
            pltpu.VMEM((3 * ch, flat + 2 * hy), BF16),
            pltpu.VMEM((2, n_all, 2, LANES), F32),
            pltpu.VMEM((2, rows, LANES), F32),
            pltpu.VMEM((2, rows // 2, LANES), F32),
            pltpu.VMEM((2, rows // 2, LANES), BF16),
            pltpu.VMEM((2, n_chips - 1, size, LANES), BF16),
            dma((3, 2)), dma((3, 2)),
            dma((2,)), dma((2,)),
            dma((2, 6)), dma((2, 6)),
        ],
        compiler_params=pltpu.CompilerParams(
            collective_id=0, has_side_effects=True, vmem_limit_bytes=48 * 2**20),
    )(
        *(pltpu.with_memory_space_constraint(value, pltpu.HBM) for value in (
            features[0], cotangent[0], occupied[0], conv_one.reshape(27 * ch, ch),
            conv_two.reshape(27 * ch, ch), gain.reshape(1, ch), shift.reshape(1, ch))))
    planes = features.shape[1:]
    so, ig, g1, g2, gg, sg = pl.pallas_call(
        functools.partial(unpack, ch, rows_half),
        out_shape=(
            jax.ShapeDtypeStruct(planes, BF16),
            jax.ShapeDtypeStruct(planes, BF16),
            jax.ShapeDtypeStruct((27 * ch, ch), F32),
            jax.ShapeDtypeStruct((27 * ch, ch), F32),
            jax.ShapeDtypeStruct((1, ch), F32),
            jax.ShapeDtypeStruct((1, ch), F32),
        ),
        in_specs=[vmem] * 4,
        out_specs=[vmem] * 6,
        compiler_params=pltpu.CompilerParams(vmem_limit_bytes=16 * 2**20),
    )(so.reshape(planes), ig.reshape(planes), q4, sums)
    shape = features.shape
    return (so.reshape(shape), ig.reshape(shape), g1.reshape(27, ch, ch),
            g2.reshape(27, ch, ch), gg.reshape(ch), sg.reshape(ch))


def solution(mesh):
    split = P("dp", None, "tile", None)
    return jax.shard_map(
        functools.partial(local, mesh.shape["dp"], mesh.shape["tile"]),
        mesh=mesh,
        in_specs=(split, P("dp", "tile", None), P(), P(), P(), P(), split),
        out_specs=(split, split, P(), P(), P(), P()),
        check_vma=False,
    )
```

```python
import functools

import jax
import jax.numpy as jnp
from jax import lax
from jax.experimental import pallas as pl
from jax.experimental.pallas import tpu as pltpu
from jax.sharding import PartitionSpec as P

BLK = 8
LANES = 128
EPSILON = 1e-05
MESH = pl.DeviceIdType.MESH
F32 = jnp.float32
BF16 = jnp.bfloat16


def kernel(
    n_dp, n_tile, ch, nx, hy,
    x_hbm, d_hbm, occ_hbm, k1_hbm, k2_hbm, gain_hbm, shift_hbm,
    so_ref, ig_ref, q4, sums_out,
    occ_ref, k1_ref, k2_ref, gain_ref, shift_ref, raw, tall, in_sem,
    w1_ref, w2_ref, w1f_ref, w2f_ref, xd_pad, a_pad, i_pad, s_x, s_d, s_t, d3, ar, part, rp, half, r1,
    halo_s, halo_r, ar_s, ar_r, rs_s, rs_r,
):
    n_z = n_tile // 2
    n_chips, n_all = n_dp * n_z, n_dp * n_tile
    dp, tile = lax.axis_index("dp"), lax.axis_index("tile")
    core, z = lax.rem(tile, 2), tile // 2
    me, chip = dp * n_tile + tile, dp * n_z + z
    flat = nx * hy
    size = r1.shape[2]
    group = n_z * size
    used = 27 * ch // 2
    blocks = -(-used // size)
    rows_core = (n_chips * size, -(-used // (2 * size)) * size)
    owners = ((min(blocks, n_chips), blocks - min(blocks, n_chips)), (rows_core[1] // size,) * 2)

    def each(count, body):
        def step(k, carry):
            body(k)
            return carry
        lax.fori_loop(1, count, step, 0, unroll=count <= 32)

    def peer(k):
        other = lax.rem(me + jnp.where(2 * me < n_all, n_all - k, k), n_all)
        return (other // n_tile, lax.rem(other, n_tile))

    def on_chip(c):
        return (c // n_z, lax.rem(c, n_z) * 2 + core)

    far_first = [
        d * n_z + k for d in reversed(range(n_dp))
        for k in sorted(range(n_z), key=lambda k: (k == 0, abs(k - n_z // 2))) if d or k]

    sibling = (dp, z * 2 + 1 - core)
    has_left, has_right = tile > 0, tile < n_tile - 1

    barrier = pltpu.get_barrier_semaphore()
    each(n_all, lambda k: pl.semaphore_signal(
        barrier, inc=1, device_id=peer(k), device_id_type=MESH))

    loads = [pltpu.make_async_copy(src, dst, in_sem.at[i]) for i, (src, dst) in enumerate((
        (occ_hbm, occ_ref), (x_hbm, raw.at[0]), (d_hbm, raw.at[1]), (k1_hbm, k1_ref),
        (k2_hbm, k2_ref), (gain_hbm, gain_ref), (shift_hbm, shift_ref)))]
    for load in loads:
        load.start()

    width = hy // BLK
    spot = lax.broadcasted_iota(jnp.int32, (1, flat), 1)
    block_x, block_y = spot // (hy * BLK), lax.rem(spot, width) // BLK
    mask = jnp.zeros((1, flat), F32)
    loads[0].wait()
    for bx in range(nx // BLK):
        for by in range(width // BLK):
            mask = jnp.where((block_x == bx) & (block_y == by),
                             occ_ref[bx, by].astype(F32), mask)
    for i in range(2):
        loads[1 + i].wait()
        tall[i] = raw[i].astype(F32).reshape(ch * nx, hy)
        for x in range(nx):
            xd_pad[pl.ds(i * ch, ch), pl.ds((x + 1) * hy, hy)] = (
                tall[i, pl.ds(x, ch, stride=nx), :] * mask[:, x * hy:(x + 1) * hy]).astype(BF16)
    for load in loads[3:]:
        load.wait()
    same = (lax.broadcasted_iota(jnp.int32, (ch, ch), 0)
            == lax.broadcasted_iota(jnp.int32, (ch, ch), 1)).astype(BF16)

    def as_matrix(taps, out):
        for a in range(3):
            out[pl.ds(a * ch, ch), :] = lax.dot_general(
                same, taps[pl.ds(a * 9 * ch, 9 * ch), :], (((1,), (1,)), ((), ())),
                preferred_element_type=F32).astype(BF16)

    def as_flipped(taps, out):
        for a in range(3):
            out[pl.ds(a * ch, ch), :] = jnp.concatenate(
                [taps[pl.ds((26 - 9 * a - k) * ch, ch), :] for k in range(9)], axis=1)

    as_matrix(k1_ref, w1_ref)

    pl.semaphore_wait(barrier, n_all - 1)

    def halo(phase, src, first, pad):
        low = pltpu.make_async_remote_copy(
            src_ref=src.at[:, pl.ds(first, hy)],
            dst_ref=pad.at[:, pl.ds(flat + hy, hy)],
            send_sem=halo_s.at[phase, 0], recv_sem=halo_r.at[phase, 0],
            device_id=(dp, tile - 1), device_id_type=MESH)
        high = pltpu.make_async_remote_copy(
            src_ref=src.at[:, pl.ds(first + flat - hy, hy)],
            dst_ref=pad.at[:, pl.ds(0, hy)],
            send_sem=halo_s.at[phase, 1], recv_sem=halo_r.at[phase, 1],
            device_id=(dp, tile + 1), device_id_type=MESH)

        @pl.when(has_left)
        def _():
            low.start()

        @pl.when(has_right)
        def _():
            high.start()

        def finish():
            @pl.when(has_left)
            def _():
                low.wait_send()
                high.wait_recv()

            @pl.when(has_right)
            def _():
                high.wait_send()
                low.wait_recv()

        return finish

    def zero_ends(pad):
        @pl.when(jnp.logical_not(has_left))
        def _():
            pad[:, pl.ds(0, hy)] = jnp.zeros((pad.shape[0], hy), pad.dtype)

        @pl.when(jnp.logical_not(has_right))
        def _():
            pad[:, pl.ds(flat + hy, hy)] = jnp.zeros((pad.shape[0], hy), pad.dtype)

    lane = lax.broadcasted_iota(jnp.int32, (1, hy), 1)
    row_h, row_y = lane // width, lax.rem(lane, width)

    def shifts(pad, first, out, inner=True, outer=True):
        def plane(x, carry):
            at = pl.ds(x * hy if isinstance(x, int) else pl.multiple_of(x * hy, hy), hy)
            values = pad[pl.ds(first, ch), at]
            for b in range(3):
                for c in range(3):
                    step = (b - 1) * width + (c - 1)
                    moved = values
                    if step:
                        moved = pltpu.roll(values, (-step) % hy, 1)
                        fits = ((row_h + (b - 1) >= 0) & (row_h + (b - 1) < BLK)
                                & (row_y + (c - 1) >= 0) & (row_y + (c - 1) < width))
                        moved = jnp.where(fits, moved, jnp.zeros_like(moved))
                    out[pl.ds((3 * b + c) * ch, ch), at] = moved.astype(BF16)
            return carry
        if inner:
            lax.fori_loop(1, nx + 1, plane, 0, unroll=True)
        if outer:
            plane(0, 0)
            plane(nx + 1, 0)

    def conv(weight, stack):
        grown = jnp.dot(weight[...], stack[...], preferred_element_type=F32)
        return (grown[:ch, :flat] + grown[ch:2 * ch, hy:hy + flat]
                + grown[2 * ch:, 2 * hy:2 * hy + flat])

    nt = (((1,), (1,)), ((), ()))

    def grad_by_input(stack, g, which):
        count = 9 * ch // 2
        side = count // 2
        first = which * rows_core[g]
        found = lax.dot_general(
            stack[span(which * count, count, 16), :], d3[...], nt, preferred_element_type=F32)
        part[g, span(first, count, 8), :] = found[:, :2 * ch]
        part[g, span(first + count, side, 8), :] = jnp.concatenate(
            [found[:side, 2 * ch:], found[side:, 2 * ch:]], axis=1)

    def grad_by_output(stack, g):
        rows = 3 * ch
        side = rows // 2
        found = lax.dot_general(d3[...], stack[...], nt, preferred_element_type=F32)
        for m in range(4):
            part[g, pl.ds(m * rows, rows), :] = found[:, m * 2 * ch:(m + 1) * 2 * ch]
        part[g, pl.ds(4 * rows, side), :] = jnp.concatenate(
            [found[:side, 8 * ch:], found[side:, 8 * ch:]], axis=1)

    def span(start, count, step):
        return pl.ds(pl.multiple_of(start, step), count)

    def put_d3(value):
        for a in range(3):
            d3[pl.ds(a * ch, ch), pl.ds(a * hy, flat)] = value

    def to_rows(columns):
        spot = lax.broadcasted_iota(jnp.int32, (ch, LANES), 1)
        block = jnp.zeros((ch, LANES), F32)
        for index, column in enumerate(columns):
            block = jnp.where(spot == index, column, block)
        return jnp.transpose(block)[:8]

    def to_columns(rows):
        return jnp.transpose(jnp.concatenate([rows, jnp.zeros((LANES - 8, ch), F32)], axis=0))

    def small_start(call, first, second, third):
        ar[call, me, 0:1, :] = jnp.concatenate([first, second], axis=1)
        ar[call, me, 1:2, :] = jnp.concatenate([third, third], axis=1)
        each(n_all, lambda k: pltpu.make_async_remote_copy(
            src_ref=ar.at[call, me], dst_ref=ar.at[call, me],
            send_sem=ar_s.at[call], recv_sem=ar_r.at[call],
            device_id=peer(k), device_id_type=MESH).start())

    def small_end(call):
        arrived = ar.at[call, pl.ds(0, n_all - 1)]
        pltpu.make_async_copy(arrived, arrived, ar_r.at[call]).wait()
        pltpu.make_async_copy(arrived, arrived, ar_s.at[call]).wait()
        return ar[call, :, 0, :], ar[call, :, 1, :]

    def merge_moments(sums_squares, counts):
        total = jnp.sum(sums_squares, axis=0, keepdims=True)
        count = jnp.sum(counts, axis=0, keepdims=True)
        off = (sums_squares / jnp.maximum(counts, 1.0) - total / jnp.maximum(count, 1.0))
        between = jnp.sum(counts * off * off, axis=0, keepdims=True)
        return jnp.concatenate(
            [total[:, :ch], total[:, ch:] + between[:, :ch], count[:, :ch],
             jnp.zeros((5, ch), F32)], axis=0)

    def by_core(g, body):
        for side in range(2):
            count = owners[g][side]
            pl.when((core == side) & (chip < count))(lambda: body(True, count))
            pl.when((core == side) & (chip >= count))(lambda: body(False, count))

    def settle(g, stage, ref):
        pltpu.make_async_copy(ref, ref, rs_r.at[g, stage]).wait()

    def drain(g, stage, ref):
        pltpu.make_async_copy(ref, ref, rs_s.at[g, stage]).wait()

    def send(g, stage, src, dst, device):
        pltpu.make_async_remote_copy(
            src_ref=src, dst_ref=dst, send_sem=rs_s.at[g, stage], recv_sem=rs_r.at[g, stage],
            device_id=device, device_id_type=MESH).start()

    def scatter_core(g):
        rows = rows_core[g]
        send(g, 0, part.at[g, span((1 - core) * rows, rows, size), :], rp.at[g, pl.ds(0, rows), :],
             sibling)

    def add_core(g):
        rows = rows_core[g]
        done = rp.at[g, pl.ds(0, rows), :]
        settle(g, 0, done)
        drain(g, 0, done)
        total = part[g, span(core * rows, rows, size), :] + rp[g, pl.ds(0, rows), :]
        rp[g, pl.ds(0, rows), :] = total
        return total

    def scatter_chips(g):
        half[g, pl.ds(0, rows_core[g]), :] = add_core(g).astype(BF16)
        here = jnp.where(core == 0, owners[g][0], owners[g][1])

        for k in far_first:
            other = lax.rem(dp + k // n_z, n_dp) * n_z + lax.rem(z + k, n_z)

            @pl.when(other < here)
            def _():
                send(g, 1, half.at[g, span(other * size, size, size), :], r1.at[g, k - 1],
                     on_chip(other))

    def sum_chips(g, owned):
        place = q4.at[g, span(core * rows_core[g] + chip * size, size, size), :]
        if owned:
            settle(g, 1, r1.at[g])
            total = rp[g, span(chip * size, size, size), :]
            for k in range(n_chips - 1):
                total = total + r1[g, k].astype(F32)
            place[...] = total.astype(BF16)
        else:
            place[...] = jnp.zeros((size, LANES), BF16)
        return place

    def drain_chips(g, owned, count):
        if count > owned:
            drain(g, 1, half.at[g, pl.ds(0, (count - owned) * size), :])

    def gather_chips(g):
        def body(owned, count):
            if owned:
                place = sum_chips(g, owned)
                each(n_chips, lambda k: send(
                    g, 2, place, place, on_chip(k - jnp.where(k > chip, 0, 1))))
        by_core(g, body)

    def gather_core(g):
        rows = rows_core[g]
        mine = q4.at[g, span(core * rows, rows, size), :]
        send(g, 3, mine, mine, sibling)

    def end_core(g):
        rows = q4.at[g, pl.ds(0, rows_core[g]), :]
        settle(g, 3, rows)
        drain(g, 3, rows)

    def end_chips(g):
        def body(owned, count):
            drain_chips(g, owned, count)
            settle(g, 2, half.at[g, pl.ds(0, (count - owned) * size), :])
            if owned:
                drain(g, 2, r1.at[g])
        by_core(g, body)

    def plane_peer(k):
        other = lax.rem(dp + k, n_dp)
        return other, (other, tile)

    def line_peer(k):
        other = lax.rem(z + k, n_z)
        return other, (dp, other * 2 + core)

    def gather_line(g):
        def body(owned, count):
            sum_chips(g, owned)
            drain_chips(g, owned, count)
        by_core(g, body)
        place = q4.at[g, span(core * rows_core[g] + chip * size, size, size), :]
        each(n_z, lambda k: send(g, 4, place, place, line_peer(k)[1]))

    def gather_plane(g):
        others = q4.at[g, pl.ds(0, (n_z - 1) * size), :]
        settle(g, 4, others)
        place = q4.at[g, span(core * rows_core[g] + dp * group, group, size), :]
        each(n_dp, lambda k: send(g, 5, place, place, plane_peer(k)[1]))
        drain(g, 4, others)

    def end_plane(g):
        others = q4.at[g, pl.ds(0, (n_dp - 1) * group), :]
        settle(g, 5, others)
        drain(g, 5, others)

    end_xd = halo(0, xd_pad, hy, xd_pad)
    shifts(xd_pad, 0, s_x, outer=False)
    zero_ends(xd_pad)
    zero_ends(a_pad)
    zero_ends(i_pad)
    inside = jnp.dot(w1_ref[...], s_x[:, pl.ds(hy, flat)], preferred_element_type=F32)
    end_xd()

    shifts(xd_pad, 0, s_x, inner=False)
    before = jnp.dot(w1_ref[pl.ds(0, ch), :], s_x[:, pl.ds(0, hy)], preferred_element_type=F32)
    after = jnp.dot(w1_ref[pl.ds(2 * ch, ch), :], s_x[:, pl.ds(hy + flat, hy)],
                    preferred_element_type=F32)
    pre = (inside[ch:2 * ch]
           + jnp.concatenate([before, inside[:ch, :flat - hy]], axis=1)
           + jnp.concatenate([inside[2 * ch:, hy:], after], axis=1))
    count_here = jnp.sum(mask, axis=1, keepdims=True)
    sums_here = jnp.sum(pre * mask, axis=1, keepdims=True)
    off = (pre - sums_here / jnp.maximum(count_here, 1.0)) * mask
    squares_here = jnp.sum(off * off, axis=1, keepdims=True)
    rows = to_rows([sums_here, squares_here])
    small_start(0, rows[0:1], rows[1:2], jnp.broadcast_to(count_here, (1, ch)))

    shifts(xd_pad, ch, s_d)
    as_flipped(k2_ref, w2f_ref)
    act_grad = conv(w2f_ref, s_d)
    gain_shift = to_columns(jnp.concatenate(
        [gain_ref[...], shift_ref[...], jnp.zeros((6, ch), F32)], axis=0))
    d3[...] = jnp.zeros(d3.shape, d3.dtype)
    for g, (first, last) in ((0, (used, 2 * rows_core[0])),
                             (1, (used // 2, rows_core[1])),
                             (1, (rows_core[1] + used // 2, 2 * rows_core[1]))):
        if last > first:
            part[g, pl.ds(first, last - first), :] = jnp.zeros((last - first, LANES), F32)
    as_matrix(k2_ref, w2_ref)
    as_flipped(k1_ref, w1f_ref)

    moments = to_columns(merge_moments(*small_end(0)))
    count = moments[:, 2:3]
    mean = moments[:, 0:1] / count
    inv_std = lax.rsqrt(moments[:, 1:2] / count + EPSILON)
    gain, shift = gain_shift[:, 0:1], gain_shift[:, 1:2]
    normal = (pre - mean) * inv_std
    pre_act = gain * normal + shift
    sg = 1.0 / (1.0 + jnp.exp(-pre_act))
    z_grad = act_grad * mask * sg * (1.0 + pre_act * (1.0 - sg))
    shift_here = jnp.sum(z_grad, axis=1, keepdims=True)
    gain_here = jnp.sum(z_grad * normal, axis=1, keepdims=True)
    rows = to_rows([shift_here, gain_here])
    small_start(1, rows[0:1], rows[1:2], rows[0:1])

    act = (pre_act * sg * mask).astype(BF16)
    a_pad[:, pl.ds(hy, flat)] = act
    end_act = halo(1, a_pad, hy, a_pad)
    put_d3(act)
    grad_by_output(s_d, 0)
    scatter_core(0)
    shifts(a_pad, 0, s_t, outer=False)
    scatter_chips(0)
    end_act()
    shifts(a_pad, 0, s_t, inner=False)
    pre_two = conv(w2_ref, s_t)
    so_ref[...] = ((xd_pad[pl.ds(0, ch), pl.ds(hy, flat)].astype(F32) + pre_two) * mask).astype(BF16)

    totals = jnp.sum(small_end(1)[0], axis=0, keepdims=True)
    totals = jnp.concatenate([totals[:, :ch], totals[:, ch:], jnp.zeros((6, ch), F32)], axis=0)
    sums_out[...] = totals
    totals = to_columns(totals)
    delta_one = (gain * inv_std * (
        z_grad - totals[:, 0:1] / count - normal * (totals[:, 1:2] / count)) * mask).astype(BF16)
    i_pad[:, pl.ds(hy, flat)] = delta_one
    end_delta = halo(2, i_pad, hy, i_pad)
    put_d3(delta_one)
    grad_by_input(s_x, 1, 1 - core)
    scatter_core(1)
    grad_by_input(s_x, 1, core)
    gather_line(0)
    scatter_chips(1)
    shifts(i_pad, 0, s_t, outer=False)
    end_delta()
    shifts(i_pad, 0, s_t, inner=False)
    back = conv(w1f_ref, s_t)
    ig_ref[...] = ((xd_pad[pl.ds(ch, ch), pl.ds(hy, flat)].astype(F32) + back) * mask).astype(BF16)
    gather_plane(0)
    gather_chips(1)
    end_plane(0)
    gather_core(0)
    end_chips(1)
    gather_core(1)
    end_core(0)
    end_core(1)


def unpack(ch, rows_core, so_in, ig_in, q4, sums, so_ref, ig_ref, g1_ref, g2_ref, gain_ref, shift_ref):
    count = 9 * ch // 2
    side = count // 2
    for core in range(2):
        first = core * rows_core
        for a in range(2):
            g1_ref[pl.ds(a * 9 * ch + core * count, count), :] = (
                q4[1, pl.ds(first, count), pl.ds(a * ch, ch)].astype(F32))
        for k in range(2):
            g1_ref[pl.ds(18 * ch + core * count + k * side, side), :] = (
                q4[1, pl.ds(first + count, side), pl.ds(k * ch, ch)].astype(F32))
    rows = 3 * ch
    half = rows // 2
    for a in range(3):
        for m in range(4):
            for side in range(2):
                g2_ref[pl.ds((26 - 9 * a - 2 * m - side) * ch, ch), :] = (
                    q4[0, pl.ds(m * rows + a * ch, ch), pl.ds(side * ch, ch)].astype(F32))
    step = ch // 2
    for part in range(6):
        side, row = part // 3, part % 3
        a, top = part // 2, part % 2
        g2_ref[pl.ds((18 - 9 * a) * ch + top * step, step), :] = (
            q4[0, pl.ds(4 * rows + row * step, step), pl.ds(side * ch, ch)].astype(F32))
    so_ref[...] = so_in[...]
    ig_ref[...] = ig_in[...]
    shift_ref[...] = sums[0:1, :]
    gain_ref[...] = sums[1:2, :]


def local(n_dp, n_tile, features, occupied, conv_one, conv_two, gain, shift, cotangent):
    scenes, ch, nx, hy = features.shape
    flat = nx * hy
    n_chips, n_all = n_dp * n_tile // 2, n_dp * n_tile
    used = 27 * ch // 2
    size = -(-used // (2 * n_chips * 16)) * 16
    rows_half = -(-used // (2 * size)) * size
    rows = 2 * n_chips * size
    vmem = pl.BlockSpec(memory_space=pltpu.VMEM)
    dma = pltpu.SemaphoreType.DMA
    so, ig, q4, sums = pl.pallas_call(
        functools.partial(kernel, n_dp, n_tile, ch, nx, hy),
        out_shape=(
            jax.ShapeDtypeStruct((ch, flat), BF16),
            jax.ShapeDtypeStruct((ch, flat), BF16),
            jax.ShapeDtypeStruct((2, rows, LANES), BF16),
            jax.ShapeDtypeStruct((8, ch), F32),
        ),
        in_specs=[pl.BlockSpec(memory_space=pltpu.HBM)] * 7,
        out_specs=[vmem] * 4,
        scratch_shapes=[
            pltpu.SMEM(occupied.shape[1:], jnp.int32),
            pltpu.VMEM((27 * ch, ch), BF16),
            pltpu.VMEM((27 * ch, ch), BF16),
            pltpu.VMEM((1, ch), F32),
            pltpu.VMEM((1, ch), F32),
            pltpu.VMEM((2, ch, nx, hy), BF16),
            pltpu.VMEM((2, ch * nx, hy), F32),
            dma((7,)),
            pltpu.VMEM((3 * ch, 9 * ch), BF16),
            pltpu.VMEM((3 * ch, 9 * ch), BF16),
            pltpu.VMEM((3 * ch, 9 * ch), BF16),
            pltpu.VMEM((3 * ch, 9 * ch), BF16),
            pltpu.VMEM((2 * ch, flat + 2 * hy), BF16),
            pltpu.VMEM((ch, flat + 2 * hy), BF16),
            pltpu.VMEM((ch, flat + 2 * hy), BF16),
            pltpu.VMEM((9 * ch, flat + 2 * hy), BF16),
            pltpu.VMEM((9 * ch, flat + 2 * hy), BF16),
            pltpu.VMEM((9 * ch, flat + 2 * hy), BF16),
            pltpu.VMEM((3 * ch, flat + 2 * hy), BF16),
            pltpu.VMEM((2, n_all, 2, LANES), F32),
            pltpu.VMEM((2, rows, LANES), F32),
            pltpu.VMEM((2, rows // 2, LANES), F32),
            pltpu.VMEM((2, rows // 2, LANES), BF16),
            pltpu.VMEM((2, n_chips - 1, size, LANES), BF16),
            dma((3, 2)), dma((3, 2)),
            dma((2,)), dma((2,)),
            dma((2, 6)), dma((2, 6)),
        ],
        compiler_params=pltpu.CompilerParams(
            collective_id=0, has_side_effects=True, vmem_limit_bytes=48 * 2**20),
    )(
        *(pltpu.with_memory_space_constraint(value, pltpu.HBM) for value in (
            features[0], cotangent[0], occupied[0], conv_one.reshape(27 * ch, ch),
            conv_two.reshape(27 * ch, ch), gain.reshape(1, ch), shift.reshape(1, ch))))
    planes = features.shape[1:]
    so, ig, g1, g2, gg, sg = pl.pallas_call(
        functools.partial(unpack, ch, rows_half),
        out_shape=(
            jax.ShapeDtypeStruct(planes, BF16),
            jax.ShapeDtypeStruct(planes, BF16),
            jax.ShapeDtypeStruct((27 * ch, ch), F32),
            jax.ShapeDtypeStruct((27 * ch, ch), F32),
            jax.ShapeDtypeStruct((1, ch), F32),
            jax.ShapeDtypeStruct((1, ch), F32),
        ),
        in_specs=[vmem] * 4,
        out_specs=[vmem] * 6,
        compiler_params=pltpu.CompilerParams(vmem_limit_bytes=16 * 2**20),
    )(so.reshape(planes), ig.reshape(planes), q4, sums)
    shape = features.shape
    return (so.reshape(shape), ig.reshape(shape), g1.reshape(27, ch, ch),
            g2.reshape(27, ch, ch), gg.reshape(ch), sg.reshape(ch))


def solution(mesh):
    split = P("dp", None, "tile", None)
    return jax.shard_map(
        functools.partial(local, mesh.shape["dp"], mesh.shape["tile"]),
        mesh=mesh,
        in_specs=(split, P("dp", "tile", None), P(), P(), P(), P(), split),
        out_specs=(split, split, P(), P(), P(), P()),
        check_vma=False,
    )
```

```python
import functools

import jax
import jax.numpy as jnp
from jax import lax
from jax.experimental import pallas as pl
from jax.experimental.pallas import tpu as pltpu
from jax.sharding import PartitionSpec as P

BLK = 8
LANES = 128
EPSILON = 1e-05
MESH = pl.DeviceIdType.MESH
F32 = jnp.float32
BF16 = jnp.bfloat16


def kernel(
    n_dp, n_tile, ch, nx, hy,
    x_hbm, d_hbm, occ_hbm, k1_hbm, k2_hbm, gain_hbm, shift_hbm,
    so_ref, ig_ref, q4, sums_out,
    occ_ref, k1_ref, k2_ref, gain_ref, shift_ref, raw, tall, in_sem,
    w1_ref, w2_ref, w1f_ref, w2f_ref, xd_pad, a_pad, i_pad, s_x, s_d, s_t, d3, ar, part, rp, half, r1,
    xs_pad, s_xs, d3s, zn, zns, pair_s, pair_r,
    halo_s, halo_r, ar_s, ar_r, rs_s, rs_r,
):
    n_z = n_tile // 2
    n_chips, n_all = n_dp * n_z, n_dp * n_tile
    dp, tile = lax.axis_index("dp"), lax.axis_index("tile")
    core, z = lax.rem(tile, 2), tile // 2
    me, chip = dp * n_tile + tile, dp * n_z + z
    flat = nx * hy
    size = r1.shape[2]
    group = n_z * size
    used = 27 * ch // 2
    blocks = -(-used // size)
    rows_core = (n_chips * size, -(-used // (2 * size)) * size)
    owners = ((min(blocks, n_chips), blocks - min(blocks, n_chips)), (rows_core[1] // size,) * 2)

    def each(count, body):
        def step(k, carry):
            body(k)
            return carry
        lax.fori_loop(1, count, step, 0, unroll=count <= 32)

    def peer(k):
        other = lax.rem(me + jnp.where(2 * me < n_all, n_all - k, k), n_all)
        return (other // n_tile, lax.rem(other, n_tile))

    def on_chip(c):
        return (c // n_z, lax.rem(c, n_z) * 2 + core)

    far_first = [
        d * n_z + k for d in reversed(range(n_dp))
        for k in sorted(range(n_z), key=lambda k: (k == 0, abs(k - n_z // 2))) if d or k]

    sibling = (dp, z * 2 + 1 - core)
    has_left, has_right = tile > 0, tile < n_tile - 1

    barrier = pltpu.get_barrier_semaphore()
    each(n_all, lambda k: pl.semaphore_signal(
        barrier, inc=1, device_id=peer(k), device_id_type=MESH))

    loads = [pltpu.make_async_copy(src, dst, in_sem.at[i]) for i, (src, dst) in enumerate((
        (occ_hbm, occ_ref), (x_hbm, raw.at[0]), (d_hbm, raw.at[1]), (k1_hbm, k1_ref),
        (k2_hbm, k2_ref), (gain_hbm, gain_ref), (shift_hbm, shift_ref)))]
    for load in loads:
        load.start()

    width = hy // BLK
    spot = lax.broadcasted_iota(jnp.int32, (1, flat), 1)
    block_x, block_y = spot // (hy * BLK), lax.rem(spot, width) // BLK
    mask = jnp.zeros((1, flat), F32)
    loads[0].wait()
    for bx in range(nx // BLK):
        for by in range(width // BLK):
            mask = jnp.where((block_x == bx) & (block_y == by),
                             occ_ref[bx, by].astype(F32), mask)
    for i in range(2):
        loads[1 + i].wait()
        tall[i] = raw[i].astype(F32).reshape(ch * nx, hy)
        for x in range(nx):
            xd_pad[pl.ds(i * ch, ch), pl.ds((x + 1) * hy, hy)] = (
                tall[i, pl.ds(x, ch, stride=nx), :] * mask[:, x * hy:(x + 1) * hy]).astype(BF16)
    for load in loads[3:]:
        load.wait()
    same = (lax.broadcasted_iota(jnp.int32, (ch, ch), 0)
            == lax.broadcasted_iota(jnp.int32, (ch, ch), 1)).astype(BF16)

    def as_matrix(taps, out):
        for a in range(3):
            out[pl.ds(a * ch, ch), :] = lax.dot_general(
                same, taps[pl.ds(a * 9 * ch, 9 * ch), :], (((1,), (1,)), ((), ())),
                preferred_element_type=F32).astype(BF16)

    def as_flipped(taps, out):
        for a in range(3):
            out[pl.ds(a * ch, ch), :] = jnp.concatenate(
                [taps[pl.ds((26 - 9 * a - k) * ch, ch), :] for k in range(9)], axis=1)

    as_matrix(k1_ref, w1_ref)

    pl.semaphore_wait(barrier, n_all - 1)

    def halo(phase, src, first, pad):
        low = pltpu.make_async_remote_copy(
            src_ref=src.at[:, pl.ds(first, hy)],
            dst_ref=pad.at[:, pl.ds(flat + hy, hy)],
            send_sem=halo_s.at[phase, 0], recv_sem=halo_r.at[phase, 0],
            device_id=(dp, tile - 1), device_id_type=MESH)
        high = pltpu.make_async_remote_copy(
            src_ref=src.at[:, pl.ds(first + flat - hy, hy)],
            dst_ref=pad.at[:, pl.ds(0, hy)],
            send_sem=halo_s.at[phase, 1], recv_sem=halo_r.at[phase, 1],
            device_id=(dp, tile + 1), device_id_type=MESH)

        @pl.when(has_left)
        def _():
            low.start()

        @pl.when(has_right)
        def _():
            high.start()

        def finish():
            @pl.when(has_left)
            def _():
                low.wait_send()
                high.wait_recv()

            @pl.when(has_right)
            def _():
                high.wait_send()
                low.wait_recv()

        return finish

    def zero_ends(pad):
        @pl.when(jnp.logical_not(has_left))
        def _():
            pad[:, pl.ds(0, hy)] = jnp.zeros((pad.shape[0], hy), pad.dtype)

        @pl.when(jnp.logical_not(has_right))
        def _():
            pad[:, pl.ds(flat + hy, hy)] = jnp.zeros((pad.shape[0], hy), pad.dtype)

    lane = lax.broadcasted_iota(jnp.int32, (1, hy), 1)
    row_h, row_y = lane // width, lax.rem(lane, width)

    def shifts(pad, first, out, inner=True, outer=True):
        def plane(x, carry):
            at = pl.ds(x * hy if isinstance(x, int) else pl.multiple_of(x * hy, hy), hy)
            values = pad[pl.ds(first, ch), at]
            for b in range(3):
                for c in range(3):
                    step = (b - 1) * width + (c - 1)
                    moved = values
                    if step:
                        moved = pltpu.roll(values, (-step) % hy, 1)
                        fits = ((row_h + (b - 1) >= 0) & (row_h + (b - 1) < BLK)
                                & (row_y + (c - 1) >= 0) & (row_y + (c - 1) < width))
                        moved = jnp.where(fits, moved, jnp.zeros_like(moved))
                    out[pl.ds((3 * b + c) * ch, ch), at] = moved.astype(BF16)
            return carry
        if inner:
            lax.fori_loop(1, nx + 1, plane, 0, unroll=True)
        if outer:
            plane(0, 0)
            plane(nx + 1, 0)

    def conv(weight, stack):
        grown = jnp.dot(weight[...], stack[...], preferred_element_type=F32)
        return (grown[:ch, :flat] + grown[ch:2 * ch, hy:hy + flat]
                + grown[2 * ch:, 2 * hy:2 * hy + flat])

    nt = (((1,), (1,)), ((), ()))

    def grad_by_input(g):
        count = 9 * ch // 2
        side = count // 2
        rows = span(core * count, count, 16)
        found = (lax.dot_general(s_x[rows, :], d3[...], nt, preferred_element_type=F32)
                 + lax.dot_general(s_xs[rows, :], d3s[...], nt, preferred_element_type=F32))
        rp[g, pl.ds(0, count), :] = found[:, :2 * ch]
        rp[g, pl.ds(count, side), :] = jnp.concatenate(
            [found[:side, 2 * ch:], found[side:, 2 * ch:]], axis=1)

    def grad_by_output(stack, g):
        rows = 3 * ch
        side = rows // 2
        found = lax.dot_general(d3[...], stack[...], nt, preferred_element_type=F32)
        for m in range(4):
            part[pl.ds(m * rows, rows), :] = found[:, m * 2 * ch:(m + 1) * 2 * ch]
        part[pl.ds(4 * rows, side), :] = jnp.concatenate(
            [found[:side, 8 * ch:], found[side:, 8 * ch:]], axis=1)

    def span(start, count, step):
        return pl.ds(pl.multiple_of(start, step), count)

    def put_d3(value, out):
        for a in range(3):
            out[pl.ds(a * ch, ch), pl.ds(a * hy, flat)] = value

    def to_rows(columns):
        spot = lax.broadcasted_iota(jnp.int32, (ch, LANES), 1)
        block = jnp.zeros((ch, LANES), F32)
        for index, column in enumerate(columns):
            block = jnp.where(spot == index, column, block)
        return jnp.transpose(block)[:8]

    def to_columns(rows):
        return jnp.transpose(jnp.concatenate([rows, jnp.zeros((LANES - 8, ch), F32)], axis=0))

    def small_start(call, first, second, third):
        ar[call, me, 0:1, :] = jnp.concatenate([first, second], axis=1)
        ar[call, me, 1:2, :] = jnp.concatenate([third, third], axis=1)
        each(n_all, lambda k: pltpu.make_async_remote_copy(
            src_ref=ar.at[call, me], dst_ref=ar.at[call, me],
            send_sem=ar_s.at[call], recv_sem=ar_r.at[call],
            device_id=peer(k), device_id_type=MESH).start())

    def small_end(call):
        arrived = ar.at[call, pl.ds(0, n_all - 1)]
        pltpu.make_async_copy(arrived, arrived, ar_r.at[call]).wait()
        pltpu.make_async_copy(arrived, arrived, ar_s.at[call]).wait()
        return ar[call, :, 0, :], ar[call, :, 1, :]

    def merge_moments(sums_squares, counts):
        total = jnp.sum(sums_squares, axis=0, keepdims=True)
        count = jnp.sum(counts, axis=0, keepdims=True)
        off = (sums_squares / jnp.maximum(counts, 1.0) - total / jnp.maximum(count, 1.0))
        between = jnp.sum(counts * off * off, axis=0, keepdims=True)
        return jnp.concatenate(
            [total[:, :ch], total[:, ch:] + between[:, :ch], count[:, :ch],
             jnp.zeros((5, ch), F32)], axis=0)

    def by_core(g, body):
        for side in range(2):
            count = owners[g][side]
            pl.when((core == side) & (chip < count))(lambda: body(True, count))
            pl.when((core == side) & (chip >= count))(lambda: body(False, count))

    def settle(g, stage, ref):
        pltpu.make_async_copy(ref, ref, rs_r.at[g, stage]).wait()

    def drain(g, stage, ref):
        pltpu.make_async_copy(ref, ref, rs_s.at[g, stage]).wait()

    def send(g, stage, src, dst, device):
        pltpu.make_async_remote_copy(
            src_ref=src, dst_ref=dst, send_sem=rs_s.at[g, stage], recv_sem=rs_r.at[g, stage],
            device_id=device, device_id_type=MESH).start()

    def scatter_core(g):
        rows = rows_core[g]
        send(g, 0, part.at[span((1 - core) * rows, rows, size), :], rp.at[g, pl.ds(0, rows), :],
             sibling)

    def pair(index, src, dst):
        return pltpu.make_async_remote_copy(
            src_ref=src, dst_ref=dst, send_sem=pair_s.at[index], recv_sem=pair_r.at[index],
            device_id=sibling, device_id_type=MESH)

    def add_core(g):
        rows = rows_core[g]
        done = rp.at[g, pl.ds(0, rows), :]
        settle(g, 0, done)
        drain(g, 0, done)
        total = part[span(core * rows, rows, size), :] + rp[g, pl.ds(0, rows), :]
        rp[g, pl.ds(0, rows), :] = total

    def scatter_chips(g):
        half[g, pl.ds(0, rows_core[g]), :] = rp[g, pl.ds(0, rows_core[g]), :].astype(BF16)
        here = jnp.where(core == 0, owners[g][0], owners[g][1])

        for k in far_first:
            other = lax.rem(dp + k // n_z, n_dp) * n_z + lax.rem(z + k, n_z)

            @pl.when(other < here)
            def _():
                send(g, 1, half.at[g, span(other * size, size, size), :], r1.at[g, k - 1],
                     on_chip(other))

    def sum_chips(g, owned):
        place = q4.at[g, span(core * rows_core[g] + chip * size, size, size), :]
        if owned:
            settle(g, 1, r1.at[g])
            total = rp[g, span(chip * size, size, size), :]
            for k in range(n_chips - 1):
                total = total + r1[g, k].astype(F32)
            place[...] = total.astype(BF16)
        else:
            place[...] = jnp.zeros((size, LANES), BF16)
        return place

    def drain_chips(g, owned, count):
        if count > owned:
            drain(g, 1, half.at[g, pl.ds(0, (count - owned) * size), :])

    def gather_chips(g):
        def body(owned, count):
            if owned:
                place = sum_chips(g, owned)
                each(n_chips, lambda k: send(
                    g, 2, place, place, on_chip(k - jnp.where(k > chip, 0, 1))))
        by_core(g, body)

    def gather_core(g):
        rows = rows_core[g]
        mine = q4.at[g, span(core * rows, rows, size), :]
        send(g, 3, mine, mine, sibling)

    def end_core(g):
        rows = q4.at[g, pl.ds(0, rows_core[g]), :]
        settle(g, 3, rows)
        drain(g, 3, rows)

    def end_chips(g):
        def body(owned, count):
            drain_chips(g, owned, count)
            settle(g, 2, half.at[g, pl.ds(0, (count - owned) * size), :])
            if owned:
                drain(g, 2, r1.at[g])
        by_core(g, body)

    def plane_peer(k):
        other = lax.rem(dp + k, n_dp)
        return other, (other, tile)

    def line_peer(k):
        other = lax.rem(z + k, n_z)
        return other, (dp, other * 2 + core)

    def gather_line(g):
        def body(owned, count):
            sum_chips(g, owned)
            drain_chips(g, owned, count)
        by_core(g, body)
        place = q4.at[g, span(core * rows_core[g] + chip * size, size, size), :]
        each(n_z, lambda k: send(g, 4, place, place, line_peer(k)[1]))

    def gather_plane(g):
        others = q4.at[g, pl.ds(0, (n_z - 1) * size), :]
        settle(g, 4, others)
        place = q4.at[g, span(core * rows_core[g] + dp * group, group, size), :]
        each(n_dp, lambda k: send(g, 5, place, place, plane_peer(k)[1]))
        drain(g, 4, others)

    def end_plane(g):
        others = q4.at[g, pl.ds(0, (n_dp - 1) * group), :]
        settle(g, 5, others)
        drain(g, 5, others)

    end_xd = halo(0, xd_pad, hy, xd_pad)
    shifts(xd_pad, 0, s_x, outer=False)
    zero_ends(xd_pad)
    zero_ends(a_pad)
    zero_ends(i_pad)
    inside = jnp.dot(w1_ref[...], s_x[:, pl.ds(hy, flat)], preferred_element_type=F32)
    end_xd()

    shifts(xd_pad, 0, s_x, inner=False)
    before = jnp.dot(w1_ref[pl.ds(0, ch), :], s_x[:, pl.ds(0, hy)], preferred_element_type=F32)
    after = jnp.dot(w1_ref[pl.ds(2 * ch, ch), :], s_x[:, pl.ds(hy + flat, hy)],
                    preferred_element_type=F32)
    pre = (inside[ch:2 * ch]
           + jnp.concatenate([before, inside[:ch, :flat - hy]], axis=1)
           + jnp.concatenate([inside[2 * ch:, hy:], after], axis=1))
    count_here = jnp.sum(mask, axis=1, keepdims=True)
    sums_here = jnp.sum(pre * mask, axis=1, keepdims=True)
    off = (pre - sums_here / jnp.maximum(count_here, 1.0)) * mask
    squares_here = jnp.sum(off * off, axis=1, keepdims=True)
    rows = to_rows([sums_here, squares_here])
    small_start(0, rows[0:1], rows[1:2], jnp.broadcast_to(count_here, (1, ch)))

    pair_x = pair(0, xd_pad.at[pl.ds(0, ch), :], xs_pad)
    pair_x.start()
    shifts(xd_pad, ch, s_d)
    as_flipped(k2_ref, w2f_ref)
    act_grad = conv(w2f_ref, s_d)
    gain_shift = to_columns(jnp.concatenate(
        [gain_ref[...], shift_ref[...], jnp.zeros((6, ch), F32)], axis=0))
    d3[...] = jnp.zeros(d3.shape, d3.dtype)
    d3s[...] = jnp.zeros(d3s.shape, d3s.dtype)
    if part.shape[0] > used:
        part[pl.ds(used, part.shape[0] - used), :] = jnp.zeros((part.shape[0] - used, LANES), F32)
    if rows_core[1] > used // 2:
        rp[1, pl.ds(used // 2, rows_core[1] - used // 2), :] = jnp.zeros(
            (rows_core[1] - used // 2, LANES), F32)
    as_matrix(k2_ref, w2_ref)
    as_flipped(k1_ref, w1f_ref)

    pair_x.wait()
    shifts(xs_pad, 0, s_xs)

    moments = to_columns(merge_moments(*small_end(0)))
    count = moments[:, 2:3]
    mean = moments[:, 0:1] / count
    inv_std = lax.rsqrt(moments[:, 1:2] / count + EPSILON)
    gain, shift = gain_shift[:, 0:1], gain_shift[:, 1:2]
    normal = (pre - mean) * inv_std
    pre_act = gain * normal + shift
    sg = 1.0 / (1.0 + jnp.exp(-pre_act))
    z_grad = act_grad * mask * sg * (1.0 + pre_act * (1.0 - sg))
    shift_here = jnp.sum(z_grad, axis=1, keepdims=True)
    gain_here = jnp.sum(z_grad * normal, axis=1, keepdims=True)
    rows = to_rows([shift_here, gain_here])
    small_start(1, rows[0:1], rows[1:2], rows[0:1])

    zn[pl.ds(0, ch), :] = z_grad
    zn[pl.ds(ch, ch), :] = normal
    zn[pl.ds(2 * ch, 8), :] = jnp.broadcast_to(mask, (8, flat))
    pair_z = pair(1, zn, zns)
    pair_z.start()
    act = (pre_act * sg * mask).astype(BF16)
    a_pad[:, pl.ds(hy, flat)] = act
    end_act = halo(1, a_pad, hy, a_pad)
    put_d3(act, d3)
    grad_by_output(s_d, 0)
    scatter_core(0)
    shifts(a_pad, 0, s_t, outer=False)
    add_core(0)
    scatter_chips(0)
    end_act()
    shifts(a_pad, 0, s_t, inner=False)
    pre_two = conv(w2_ref, s_t)
    so_ref[...] = ((xd_pad[pl.ds(0, ch), pl.ds(hy, flat)].astype(F32) + pre_two) * mask).astype(BF16)

    totals = jnp.sum(small_end(1)[0], axis=0, keepdims=True)
    totals = jnp.concatenate([totals[:, :ch], totals[:, ch:], jnp.zeros((6, ch), F32)], axis=0)
    sums_out[...] = totals
    totals = to_columns(totals)
    def delta(z_grad, normal, mask):
        return (gain * inv_std * (
            z_grad - totals[:, 0:1] / count - normal * (totals[:, 1:2] / count)) * mask).astype(BF16)

    delta_one = delta(z_grad, normal, mask)
    i_pad[:, pl.ds(hy, flat)] = delta_one
    end_delta = halo(2, i_pad, hy, i_pad)
    put_d3(delta_one, d3)
    pair_z.wait()
    put_d3(delta(zns[pl.ds(0, ch), :], zns[pl.ds(ch, ch), :], zns[pl.ds(2 * ch, 1), :]), d3s)
    grad_by_input(1)
    scatter_chips(1)
    gather_line(0)
    shifts(i_pad, 0, s_t, outer=False)
    end_delta()
    shifts(i_pad, 0, s_t, inner=False)
    back = conv(w1f_ref, s_t)
    ig_ref[...] = ((xd_pad[pl.ds(ch, ch), pl.ds(hy, flat)].astype(F32) + back) * mask).astype(BF16)
    gather_chips(1)
    gather_plane(0)
    end_plane(0)
    gather_core(0)
    end_chips(1)
    gather_core(1)
    end_core(0)
    end_core(1)


def unpack(ch, rows_core, so_in, ig_in, q4, sums, so_ref, ig_ref, g1_ref, g2_ref, gain_ref, shift_ref):
    count = 9 * ch // 2
    side = count // 2
    for core in range(2):
        first = core * rows_core
        for a in range(2):
            g1_ref[pl.ds(a * 9 * ch + core * count, count), :] = (
                q4[1, pl.ds(first, count), pl.ds(a * ch, ch)].astype(F32))
        for k in range(2):
            g1_ref[pl.ds(18 * ch + core * count + k * side, side), :] = (
                q4[1, pl.ds(first + count, side), pl.ds(k * ch, ch)].astype(F32))
    rows = 3 * ch
    half = rows // 2
    for a in range(3):
        for m in range(4):
            for side in range(2):
                g2_ref[pl.ds((26 - 9 * a - 2 * m - side) * ch, ch), :] = (
                    q4[0, pl.ds(m * rows + a * ch, ch), pl.ds(side * ch, ch)].astype(F32))
    step = ch // 2
    for part in range(6):
        side, row = part // 3, part % 3
        a, top = part // 2, part % 2
        g2_ref[pl.ds((18 - 9 * a) * ch + top * step, step), :] = (
            q4[0, pl.ds(4 * rows + row * step, step), pl.ds(side * ch, ch)].astype(F32))
    so_ref[...] = so_in[...]
    ig_ref[...] = ig_in[...]
    shift_ref[...] = sums[0:1, :]
    gain_ref[...] = sums[1:2, :]


def local(n_dp, n_tile, features, occupied, conv_one, conv_two, gain, shift, cotangent):
    scenes, ch, nx, hy = features.shape
    flat = nx * hy
    n_chips, n_all = n_dp * n_tile // 2, n_dp * n_tile
    used = 27 * ch // 2
    size = -(-used // (2 * n_chips * 16)) * 16
    rows_half = -(-used // (2 * size)) * size
    rows = 2 * n_chips * size
    vmem = pl.BlockSpec(memory_space=pltpu.VMEM)
    dma = pltpu.SemaphoreType.DMA
    so, ig, q4, sums = pl.pallas_call(
        functools.partial(kernel, n_dp, n_tile, ch, nx, hy),
        out_shape=(
            jax.ShapeDtypeStruct((ch, flat), BF16),
            jax.ShapeDtypeStruct((ch, flat), BF16),
            jax.ShapeDtypeStruct((2, rows, LANES), BF16),
            jax.ShapeDtypeStruct((8, ch), F32),
        ),
        in_specs=[pl.BlockSpec(memory_space=pltpu.HBM)] * 7,
        out_specs=[vmem] * 4,
        scratch_shapes=[
            pltpu.SMEM(occupied.shape[1:], jnp.int32),
            pltpu.VMEM((27 * ch, ch), BF16),
            pltpu.VMEM((27 * ch, ch), BF16),
            pltpu.VMEM((1, ch), F32),
            pltpu.VMEM((1, ch), F32),
            pltpu.VMEM((2, ch, nx, hy), BF16),
            pltpu.VMEM((2, ch * nx, hy), F32),
            dma((7,)),
            pltpu.VMEM((3 * ch, 9 * ch), BF16),
            pltpu.VMEM((3 * ch, 9 * ch), BF16),
            pltpu.VMEM((3 * ch, 9 * ch), BF16),
            pltpu.VMEM((3 * ch, 9 * ch), BF16),
            pltpu.VMEM((2 * ch, flat + 2 * hy), BF16),
            pltpu.VMEM((ch, flat + 2 * hy), BF16),
            pltpu.VMEM((ch, flat + 2 * hy), BF16),
            pltpu.VMEM((9 * ch, flat + 2 * hy), BF16),
            pltpu.VMEM((9 * ch, flat + 2 * hy), BF16),
            pltpu.VMEM((9 * ch, flat + 2 * hy), BF16),
            pltpu.VMEM((3 * ch, flat + 2 * hy), BF16),
            pltpu.VMEM((2, n_all, 2, LANES), F32),
            pltpu.VMEM((rows, LANES), F32),
            pltpu.VMEM((2, rows // 2, LANES), F32),
            pltpu.VMEM((2, rows // 2, LANES), BF16),
            pltpu.VMEM((2, n_chips - 1, size, LANES), BF16),
            pltpu.VMEM((ch, flat + 2 * hy), BF16),
            pltpu.VMEM((9 * ch, flat + 2 * hy), BF16),
            pltpu.VMEM((3 * ch, flat + 2 * hy), BF16),
            pltpu.VMEM((2 * ch + 8, flat), F32),
            pltpu.VMEM((2 * ch + 8, flat), F32),
            dma((2,)), dma((2,)),
            dma((3, 2)), dma((3, 2)),
            dma((2,)), dma((2,)),
            dma((2, 6)), dma((2, 6)),
        ],
        compiler_params=pltpu.CompilerParams(
            collective_id=0, has_side_effects=True, vmem_limit_bytes=48 * 2**20),
    )(
        *(pltpu.with_memory_space_constraint(value, pltpu.HBM) for value in (
            features[0], cotangent[0], occupied[0], conv_one.reshape(27 * ch, ch),
            conv_two.reshape(27 * ch, ch), gain.reshape(1, ch), shift.reshape(1, ch))))
    planes = features.shape[1:]
    so, ig, g1, g2, gg, sg = pl.pallas_call(
        functools.partial(unpack, ch, rows_half),
        out_shape=(
            jax.ShapeDtypeStruct(planes, BF16),
            jax.ShapeDtypeStruct(planes, BF16),
            jax.ShapeDtypeStruct((27 * ch, ch), F32),
            jax.ShapeDtypeStruct((27 * ch, ch), F32),
            jax.ShapeDtypeStruct((1, ch), F32),
            jax.ShapeDtypeStruct((1, ch), F32),
        ),
        in_specs=[vmem] * 4,
        out_specs=[vmem] * 6,
        compiler_params=pltpu.CompilerParams(vmem_limit_bytes=16 * 2**20),
    )(so.reshape(planes), ig.reshape(planes), q4, sums)
    shape = features.shape
    return (so.reshape(shape), ig.reshape(shape), g1.reshape(27, ch, ch),
            g2.reshape(27, ch, ch), gg.reshape(ch), sg.reshape(ch))


def solution(mesh):
    split = P("dp", None, "tile", None)
    return jax.shard_map(
        functools.partial(local, mesh.shape["dp"], mesh.shape["tile"]),
        mesh=mesh,
        in_specs=(split, P("dp", "tile", None), P(), P(), P(), P(), split),
        out_specs=(split, split, P(), P(), P(), P()),
        check_vma=False,
    )
```

```python
import functools

import jax
import jax.numpy as jnp
from jax import lax
from jax.experimental import pallas as pl
from jax.experimental.pallas import tpu as pltpu
from jax.sharding import PartitionSpec as P

BLK = 8
LANES = 128
EPSILON = 1e-05
MESH = pl.DeviceIdType.MESH
F32 = jnp.float32
BF16 = jnp.bfloat16


def kernel(
    n_dp, n_tile, ch, nx, hy,
    x_hbm, d_hbm, occ_hbm, k1_hbm, k2_hbm, gain_hbm, shift_hbm,
    so_ref, ig_ref, q4, sums_out,
    occ_ref, k1_ref, k2_ref, gain_ref, shift_ref, raw, tall, in_sem,
    w1_ref, w2_ref, w1f_ref, w2f_ref, xd_pad, a_pad, i_pad, s_x, s_d, s_t, d3, ar, part, rp, half, r1,
    xs_pad, s_xs, d3s, zn, zns, pair_s, pair_r,
    halo_s, halo_r, ar_s, ar_r, rs_s, rs_r,
):
    n_z = n_tile // 2
    n_chips, n_all = n_dp * n_z, n_dp * n_tile
    dp, tile = lax.axis_index("dp"), lax.axis_index("tile")
    core, z = lax.rem(tile, 2), tile // 2
    me, chip = dp * n_tile + tile, dp * n_z + z
    flat = nx * hy
    size = r1.shape[2]
    group = n_z * size
    used = 27 * ch // 2
    blocks = -(-used // size)
    rows_core = (n_chips * size, -(-used // (2 * size)) * size)
    owners = ((min(blocks, n_chips), blocks - min(blocks, n_chips)), (rows_core[1] // size,) * 2)

    def each(count, body):
        def step(k, carry):
            body(k)
            return carry
        lax.fori_loop(1, count, step, 0, unroll=count <= 32)

    def peer(k):
        other = lax.rem(me + jnp.where(2 * me < n_all, n_all - k, k), n_all)
        return (other // n_tile, lax.rem(other, n_tile))

    def on_chip(c):
        return (c // n_z, lax.rem(c, n_z) * 2 + core)

    far_first = [
        d * n_z + k for d in reversed(range(n_dp))
        for k in sorted(range(n_z), key=lambda k: (k == 0, abs(k - n_z // 2))) if d or k]

    sibling = (dp, z * 2 + 1 - core)
    has_left, has_right = tile > 0, tile < n_tile - 1

    barrier = pltpu.get_barrier_semaphore()
    each(n_all, lambda k: pl.semaphore_signal(
        barrier, inc=1, device_id=peer(k), device_id_type=MESH))

    loads = [pltpu.make_async_copy(src, dst, in_sem.at[i]) for i, (src, dst) in enumerate((
        (occ_hbm, occ_ref), (x_hbm, raw.at[0]), (d_hbm, raw.at[1]), (k1_hbm, k1_ref),
        (k2_hbm, k2_ref), (gain_hbm, gain_ref), (shift_hbm, shift_ref)))]
    for load in loads:
        load.start()

    width = hy // BLK
    spot = lax.broadcasted_iota(jnp.int32, (1, flat), 1)
    block_x, block_y = spot // (hy * BLK), lax.rem(spot, width) // BLK
    mask = jnp.zeros((1, flat), F32)
    loads[0].wait()
    for bx in range(nx // BLK):
        for by in range(width // BLK):
            mask = jnp.where((block_x == bx) & (block_y == by),
                             occ_ref[bx, by].astype(F32), mask)
    for i in range(2):
        loads[1 + i].wait()
        tall[i] = raw[i].astype(F32).reshape(ch * nx, hy)
        for x in range(nx):
            xd_pad[pl.ds(i * ch, ch), pl.ds((x + 1) * hy, hy)] = (
                tall[i, pl.ds(x, ch, stride=nx), :] * mask[:, x * hy:(x + 1) * hy]).astype(BF16)
    for load in loads[3:]:
        load.wait()
    same = (lax.broadcasted_iota(jnp.int32, (ch, ch), 0)
            == lax.broadcasted_iota(jnp.int32, (ch, ch), 1)).astype(BF16)

    def as_matrix(taps, out):
        for a in range(3):
            out[pl.ds(a * ch, ch), :] = lax.dot_general(
                same, taps[pl.ds(a * 9 * ch, 9 * ch), :], (((1,), (1,)), ((), ())),
                preferred_element_type=F32).astype(BF16)

    def as_flipped(taps, out):
        for a in range(3):
            out[pl.ds(a * ch, ch), :] = jnp.concatenate(
                [taps[pl.ds((26 - 9 * a - k) * ch, ch), :] for k in range(9)], axis=1)

    as_matrix(k1_ref, w1_ref)

    pl.semaphore_wait(barrier, n_all - 1)

    def halo(phase, src, first, pad):
        low = pltpu.make_async_remote_copy(
            src_ref=src.at[:, pl.ds(first, hy)],
            dst_ref=pad.at[:, pl.ds(flat + hy, hy)],
            send_sem=halo_s.at[phase, 0], recv_sem=halo_r.at[phase, 0],
            device_id=(dp, tile - 1), device_id_type=MESH)
        high = pltpu.make_async_remote_copy(
            src_ref=src.at[:, pl.ds(first + flat - hy, hy)],
            dst_ref=pad.at[:, pl.ds(0, hy)],
            send_sem=halo_s.at[phase, 1], recv_sem=halo_r.at[phase, 1],
            device_id=(dp, tile + 1), device_id_type=MESH)

        @pl.when(has_left)
        def _():
            low.start()

        @pl.when(has_right)
        def _():
            high.start()

        def finish():
            @pl.when(has_left)
            def _():
                low.wait_send()
                high.wait_recv()

            @pl.when(has_right)
            def _():
                high.wait_send()
                low.wait_recv()

        return finish

    def zero_ends(pad):
        @pl.when(jnp.logical_not(has_left))
        def _():
            pad[:, pl.ds(0, hy)] = jnp.zeros((pad.shape[0], hy), pad.dtype)

        @pl.when(jnp.logical_not(has_right))
        def _():
            pad[:, pl.ds(flat + hy, hy)] = jnp.zeros((pad.shape[0], hy), pad.dtype)

    lane = lax.broadcasted_iota(jnp.int32, (1, hy), 1)
    row_h, row_y = lane // width, lax.rem(lane, width)

    def shifts(pad, first, out, inner=True, outer=True):
        def plane(x, carry):
            at = pl.ds(x * hy if isinstance(x, int) else pl.multiple_of(x * hy, hy), hy)
            values = pad[pl.ds(first, ch), at]
            for b in range(3):
                for c in range(3):
                    step = (b - 1) * width + (c - 1)
                    moved = values
                    if step:
                        moved = pltpu.roll(values, (-step) % hy, 1)
                        fits = ((row_h + (b - 1) >= 0) & (row_h + (b - 1) < BLK)
                                & (row_y + (c - 1) >= 0) & (row_y + (c - 1) < width))
                        moved = jnp.where(fits, moved, jnp.zeros_like(moved))
                    out[pl.ds((3 * b + c) * ch, ch), at] = moved.astype(BF16)
            return carry
        if inner:
            lax.fori_loop(1, nx + 1, plane, 0, unroll=True)
        if outer:
            plane(0, 0)
            plane(nx + 1, 0)

    def conv(weight, stack):
        grown = jnp.dot(weight[...], stack[...], preferred_element_type=F32)
        return (grown[:ch, :flat] + grown[ch:2 * ch, hy:hy + flat]
                + grown[2 * ch:, 2 * hy:2 * hy + flat])

    nt = (((1,), (1,)), ((), ()))

    def grad_by_input(g):
        count = 9 * ch // 2
        side = count // 2
        rows = span(core * count, count, 16)
        found = (lax.dot_general(s_x[rows, :], d3[...], nt, preferred_element_type=F32)
                 + lax.dot_general(s_xs[rows, :], d3s[...], nt, preferred_element_type=F32))
        rp[g, pl.ds(0, count), :] = found[:, :2 * ch]
        rp[g, pl.ds(count, side), :] = jnp.concatenate(
            [found[:side, 2 * ch:], found[side:, 2 * ch:]], axis=1)

    def grad_by_output(stack, g):
        rows = 3 * ch
        side = rows // 2
        found = lax.dot_general(d3[...], stack[...], nt, preferred_element_type=F32)
        for m in range(4):
            part[pl.ds(m * rows, rows), :] = found[:, m * 2 * ch:(m + 1) * 2 * ch]
        part[pl.ds(4 * rows, side), :] = jnp.concatenate(
            [found[:side, 8 * ch:], found[side:, 8 * ch:]], axis=1)

    def span(start, count, step):
        return pl.ds(pl.multiple_of(start, step), count)

    def put_d3(value, out):
        for a in range(3):
            out[pl.ds(a * ch, ch), pl.ds(a * hy, flat)] = value

    def to_rows(columns):
        spot = lax.broadcasted_iota(jnp.int32, (ch, LANES), 1)
        block = jnp.zeros((ch, LANES), F32)
        for index, column in enumerate(columns):
            block = jnp.where(spot == index, column, block)
        return jnp.transpose(block)[:8]

    def to_columns(rows):
        return jnp.transpose(jnp.concatenate([rows, jnp.zeros((LANES - 8, ch), F32)], axis=0))

    def small_start(call, first, second):
        ar[call, me] = jnp.concatenate([first, second], axis=1)
        each(n_all, lambda k: pltpu.make_async_remote_copy(
            src_ref=ar.at[call, me], dst_ref=ar.at[call, me],
            send_sem=ar_s.at[call], recv_sem=ar_r.at[call],
            device_id=peer(k), device_id_type=MESH).start())

    def small_end(call):
        arrived = ar.at[call, pl.ds(0, n_all - 1)]
        pltpu.make_async_copy(arrived, arrived, ar_r.at[call]).wait()
        pltpu.make_async_copy(arrived, arrived, ar_s.at[call]).wait()
        return ar[call, :, 0, :]

    def merge_moments(sums_squares, counts):
        total = jnp.sum(sums_squares, axis=0, keepdims=True)
        count = jnp.sum(counts, axis=0, keepdims=True)
        off = (sums_squares / jnp.maximum(counts, 1.0) - total / jnp.maximum(count, 1.0))
        between = jnp.sum(counts * off * off, axis=0, keepdims=True)
        return jnp.concatenate(
            [total[:, :ch], total[:, ch:] + between[:, :ch], count[:, :ch],
             jnp.zeros((5, ch), F32)], axis=0)

    def by_core(g, body):
        for side in range(2):
            count = owners[g][side]
            pl.when((core == side) & (chip < count))(lambda: body(True, count))
            pl.when((core == side) & (chip >= count))(lambda: body(False, count))

    def settle(g, stage, ref):
        pltpu.make_async_copy(ref, ref, rs_r.at[g, stage]).wait()

    def drain(g, stage, ref):
        pltpu.make_async_copy(ref, ref, rs_s.at[g, stage]).wait()

    def send(g, stage, src, dst, device):
        pltpu.make_async_remote_copy(
            src_ref=src, dst_ref=dst, send_sem=rs_s.at[g, stage], recv_sem=rs_r.at[g, stage],
            device_id=device, device_id_type=MESH).start()

    def scatter_core(g):
        rows = rows_core[g]
        send(g, 0, part.at[span((1 - core) * rows, rows, size), :], rp.at[g, pl.ds(0, rows), :],
             sibling)

    def pair(index, src, dst):
        return pltpu.make_async_remote_copy(
            src_ref=src, dst_ref=dst, send_sem=pair_s.at[index], recv_sem=pair_r.at[index],
            device_id=sibling, device_id_type=MESH)

    def add_core(g):
        rows = rows_core[g]
        done = rp.at[g, pl.ds(0, rows), :]
        settle(g, 0, done)
        drain(g, 0, done)
        total = part[span(core * rows, rows, size), :] + rp[g, pl.ds(0, rows), :]
        rp[g, pl.ds(0, rows), :] = total

    def scatter_chips(g):
        half[g, pl.ds(0, rows_core[g]), :] = rp[g, pl.ds(0, rows_core[g]), :].astype(BF16)
        here = jnp.where(core == 0, owners[g][0], owners[g][1])

        for k in far_first:
            other = lax.rem(dp + k // n_z, n_dp) * n_z + lax.rem(z + k, n_z)

            @pl.when(other < here)
            def _():
                send(g, 1, half.at[g, span(other * size, size, size), :], r1.at[g, k - 1],
                     on_chip(other))

    def sum_chips(g, owned):
        place = q4.at[g, span(core * rows_core[g] + chip * size, size, size), :]
        if owned:
            settle(g, 1, r1.at[g])
            total = rp[g, span(chip * size, size, size), :]
            for k in range(n_chips - 1):
                total = total + r1[g, k].astype(F32)
            place[...] = total.astype(BF16)
        else:
            place[...] = jnp.zeros((size, LANES), BF16)
        return place

    def drain_chips(g, owned, count):
        if count > owned:
            drain(g, 1, half.at[g, pl.ds(0, (count - owned) * size), :])

    def gather_chips(g):
        def body(owned, count):
            if owned:
                place = sum_chips(g, owned)
                each(n_chips, lambda k: send(
                    g, 2, place, place, on_chip(k - jnp.where(k > chip, 0, 1))))
        by_core(g, body)

    def gather_core(g):
        rows = rows_core[g]
        mine = q4.at[g, span(core * rows, rows, size), :]
        send(g, 3, mine, mine, sibling)

    def end_core(g):
        rows = q4.at[g, pl.ds(0, rows_core[g]), :]
        settle(g, 3, rows)
        drain(g, 3, rows)

    def end_chips(g):
        def body(owned, count):
            drain_chips(g, owned, count)
            settle(g, 2, half.at[g, pl.ds(0, (count - owned) * size), :])
            if owned:
                drain(g, 2, r1.at[g])
        by_core(g, body)

    def plane_peer(k):
        other = lax.rem(dp + k, n_dp)
        return other, (other, tile)

    def line_peer(k):
        other = lax.rem(z + k, n_z)
        return other, (dp, other * 2 + core)

    def gather_line(g):
        def body(owned, count):
            sum_chips(g, owned)
            drain_chips(g, owned, count)
        by_core(g, body)
        place = q4.at[g, span(core * rows_core[g] + chip * size, size, size), :]
        each(n_z, lambda k: send(g, 4, place, place, line_peer(k)[1]))

    def gather_plane(g):
        others = q4.at[g, pl.ds(0, (n_z - 1) * size), :]
        settle(g, 4, others)
        place = q4.at[g, span(core * rows_core[g] + dp * group, group, size), :]
        each(n_dp, lambda k: send(g, 5, place, place, plane_peer(k)[1]))
        drain(g, 4, others)

    def end_plane(g):
        others = q4.at[g, pl.ds(0, (n_dp - 1) * group), :]
        settle(g, 5, others)
        drain(g, 5, others)

    end_xd = halo(0, xd_pad, hy, xd_pad)
    count_here = jnp.sum(mask, axis=1, keepdims=True)
    counts = jnp.broadcast_to(count_here, (1, ch))
    small_start(2, counts, counts)
    shifts(xd_pad, 0, s_x, outer=False)
    zero_ends(xd_pad)
    zero_ends(a_pad)
    zero_ends(i_pad)
    inside = jnp.dot(w1_ref[...], s_x[:, pl.ds(hy, flat)], preferred_element_type=F32)
    end_xd()

    shifts(xd_pad, 0, s_x, inner=False)
    before = jnp.dot(w1_ref[pl.ds(0, ch), :], s_x[:, pl.ds(0, hy)], preferred_element_type=F32)
    after = jnp.dot(w1_ref[pl.ds(2 * ch, ch), :], s_x[:, pl.ds(hy + flat, hy)],
                    preferred_element_type=F32)
    pre = (inside[ch:2 * ch]
           + jnp.concatenate([before, inside[:ch, :flat - hy]], axis=1)
           + jnp.concatenate([inside[2 * ch:, hy:], after], axis=1))
    sums_here = jnp.sum(pre * mask, axis=1, keepdims=True)
    off = (pre - sums_here / jnp.maximum(count_here, 1.0)) * mask
    squares_here = jnp.sum(off * off, axis=1, keepdims=True)
    rows = to_rows([sums_here, squares_here])
    small_start(0, rows[0:1], rows[1:2])

    pair_x = pair(0, xd_pad.at[pl.ds(0, ch), :], xs_pad)
    pair_x.start()
    shifts(xd_pad, ch, s_d)
    as_flipped(k2_ref, w2f_ref)
    act_grad = conv(w2f_ref, s_d)
    gain_shift = to_columns(jnp.concatenate(
        [gain_ref[...], shift_ref[...], jnp.zeros((6, ch), F32)], axis=0))
    d3[...] = jnp.zeros(d3.shape, d3.dtype)
    d3s[...] = jnp.zeros(d3s.shape, d3s.dtype)
    if part.shape[0] > used:
        part[pl.ds(used, part.shape[0] - used), :] = jnp.zeros((part.shape[0] - used, LANES), F32)
    if rows_core[1] > used // 2:
        rp[1, pl.ds(used // 2, rows_core[1] - used // 2), :] = jnp.zeros(
            (rows_core[1] - used // 2, LANES), F32)
    as_matrix(k2_ref, w2_ref)
    as_flipped(k1_ref, w1f_ref)

    pair_x.wait()
    shifts(xs_pad, 0, s_xs)

    moments = to_columns(merge_moments(small_end(0), small_end(2)))
    count = moments[:, 2:3]
    mean = moments[:, 0:1] / count
    inv_std = lax.rsqrt(moments[:, 1:2] / count + EPSILON)
    gain, shift = gain_shift[:, 0:1], gain_shift[:, 1:2]
    normal = (pre - mean) * inv_std
    pre_act = gain * normal + shift
    sg = 1.0 / (1.0 + jnp.exp(-pre_act))
    z_grad = act_grad * mask * sg * (1.0 + pre_act * (1.0 - sg))
    shift_here = jnp.sum(z_grad, axis=1, keepdims=True)
    gain_here = jnp.sum(z_grad * normal, axis=1, keepdims=True)
    rows = to_rows([shift_here, gain_here])
    small_start(1, rows[0:1], rows[1:2])

    zn[pl.ds(0, ch), :] = z_grad
    zn[pl.ds(ch, ch), :] = normal
    zn[pl.ds(2 * ch, 8), :] = jnp.broadcast_to(mask, (8, flat))
    pair_z = pair(1, zn, zns)
    pair_z.start()
    act = (pre_act * sg * mask).astype(BF16)
    a_pad[:, pl.ds(hy, flat)] = act
    end_act = halo(1, a_pad, hy, a_pad)
    put_d3(act, d3)
    grad_by_output(s_d, 0)
    scatter_core(0)
    shifts(a_pad, 0, s_t, outer=False)
    add_core(0)
    scatter_chips(0)
    end_act()
    shifts(a_pad, 0, s_t, inner=False)
    pre_two = conv(w2_ref, s_t)
    so_ref[...] = ((xd_pad[pl.ds(0, ch), pl.ds(hy, flat)].astype(F32) + pre_two) * mask).astype(BF16)

    totals = jnp.sum(small_end(1), axis=0, keepdims=True)
    totals = jnp.concatenate([totals[:, :ch], totals[:, ch:], jnp.zeros((6, ch), F32)], axis=0)
    sums_out[...] = totals
    totals = to_columns(totals)
    def delta(z_grad, normal, mask):
        return (gain * inv_std * (
            z_grad - totals[:, 0:1] / count - normal * (totals[:, 1:2] / count)) * mask).astype(BF16)

    delta_one = delta(z_grad, normal, mask)
    i_pad[:, pl.ds(hy, flat)] = delta_one
    end_delta = halo(2, i_pad, hy, i_pad)
    put_d3(delta_one, d3)
    pair_z.wait()
    put_d3(delta(zns[pl.ds(0, ch), :], zns[pl.ds(ch, ch), :], zns[pl.ds(2 * ch, 1), :]), d3s)
    grad_by_input(1)
    scatter_chips(1)
    gather_line(0)
    shifts(i_pad, 0, s_t, outer=False)
    end_delta()
    shifts(i_pad, 0, s_t, inner=False)
    back = conv(w1f_ref, s_t)
    ig_ref[...] = ((xd_pad[pl.ds(ch, ch), pl.ds(hy, flat)].astype(F32) + back) * mask).astype(BF16)
    gather_chips(1)
    gather_plane(0)
    end_plane(0)
    gather_core(0)
    end_chips(1)
    gather_core(1)
    end_core(0)
    end_core(1)


def unpack(ch, rows_core, so_in, ig_in, q4, sums, so_ref, ig_ref, g1_ref, g2_ref, gain_ref, shift_ref):
    count = 9 * ch // 2
    side = count // 2
    for core in range(2):
        first = core * rows_core
        for a in range(2):
            g1_ref[pl.ds(a * 9 * ch + core * count, count), :] = (
                q4[1, pl.ds(first, count), pl.ds(a * ch, ch)].astype(F32))
        for k in range(2):
            g1_ref[pl.ds(18 * ch + core * count + k * side, side), :] = (
                q4[1, pl.ds(first + count, side), pl.ds(k * ch, ch)].astype(F32))
    rows = 3 * ch
    half = rows // 2
    for a in range(3):
        for m in range(4):
            for side in range(2):
                g2_ref[pl.ds((26 - 9 * a - 2 * m - side) * ch, ch), :] = (
                    q4[0, pl.ds(m * rows + a * ch, ch), pl.ds(side * ch, ch)].astype(F32))
    step = ch // 2
    for part in range(6):
        side, row = part // 3, part % 3
        a, top = part // 2, part % 2
        g2_ref[pl.ds((18 - 9 * a) * ch + top * step, step), :] = (
            q4[0, pl.ds(4 * rows + row * step, step), pl.ds(side * ch, ch)].astype(F32))
    so_ref[...] = so_in[...]
    ig_ref[...] = ig_in[...]
    shift_ref[...] = sums[0:1, :]
    gain_ref[...] = sums[1:2, :]


def local(n_dp, n_tile, features, occupied, conv_one, conv_two, gain, shift, cotangent):
    scenes, ch, nx, hy = features.shape
    flat = nx * hy
    n_chips, n_all = n_dp * n_tile // 2, n_dp * n_tile
    used = 27 * ch // 2
    size = -(-used // (2 * n_chips * 16)) * 16
    rows_half = -(-used // (2 * size)) * size
    rows = 2 * n_chips * size
    vmem = pl.BlockSpec(memory_space=pltpu.VMEM)
    dma = pltpu.SemaphoreType.DMA
    so, ig, q4, sums = pl.pallas_call(
        functools.partial(kernel, n_dp, n_tile, ch, nx, hy),
        out_shape=(
            jax.ShapeDtypeStruct((ch, flat), BF16),
            jax.ShapeDtypeStruct((ch, flat), BF16),
            jax.ShapeDtypeStruct((2, rows, LANES), BF16),
            jax.ShapeDtypeStruct((8, ch), F32),
        ),
        in_specs=[pl.BlockSpec(memory_space=pltpu.HBM)] * 7,
        out_specs=[vmem] * 4,
        scratch_shapes=[
            pltpu.SMEM(occupied.shape[1:], jnp.int32),
            pltpu.VMEM((27 * ch, ch), BF16),
            pltpu.VMEM((27 * ch, ch), BF16),
            pltpu.VMEM((1, ch), F32),
            pltpu.VMEM((1, ch), F32),
            pltpu.VMEM((2, ch, nx, hy), BF16),
            pltpu.VMEM((2, ch * nx, hy), F32),
            dma((7,)),
            pltpu.VMEM((3 * ch, 9 * ch), BF16),
            pltpu.VMEM((3 * ch, 9 * ch), BF16),
            pltpu.VMEM((3 * ch, 9 * ch), BF16),
            pltpu.VMEM((3 * ch, 9 * ch), BF16),
            pltpu.VMEM((2 * ch, flat + 2 * hy), BF16),
            pltpu.VMEM((ch, flat + 2 * hy), BF16),
            pltpu.VMEM((ch, flat + 2 * hy), BF16),
            pltpu.VMEM((9 * ch, flat + 2 * hy), BF16),
            pltpu.VMEM((9 * ch, flat + 2 * hy), BF16),
            pltpu.VMEM((9 * ch, flat + 2 * hy), BF16),
            pltpu.VMEM((3 * ch, flat + 2 * hy), BF16),
            pltpu.VMEM((3, n_all, 1, LANES), F32),
            pltpu.VMEM((rows, LANES), F32),
            pltpu.VMEM((2, rows // 2, LANES), F32),
            pltpu.VMEM((2, rows // 2, LANES), BF16),
            pltpu.VMEM((2, n_chips - 1, size, LANES), BF16),
            pltpu.VMEM((ch, flat + 2 * hy), BF16),
            pltpu.VMEM((9 * ch, flat + 2 * hy), BF16),
            pltpu.VMEM((3 * ch, flat + 2 * hy), BF16),
            pltpu.VMEM((2 * ch + 8, flat), F32),
            pltpu.VMEM((2 * ch + 8, flat), F32),
            dma((2,)), dma((2,)),
            dma((3, 2)), dma((3, 2)),
            dma((3,)), dma((3,)),
            dma((2, 6)), dma((2, 6)),
        ],
        compiler_params=pltpu.CompilerParams(
            collective_id=0, has_side_effects=True, vmem_limit_bytes=48 * 2**20),
    )(
        *(pltpu.with_memory_space_constraint(value, pltpu.HBM) for value in (
            features[0], cotangent[0], occupied[0], conv_one.reshape(27 * ch, ch),
            conv_two.reshape(27 * ch, ch), gain.reshape(1, ch), shift.reshape(1, ch))))
    planes = features.shape[1:]
    so, ig, g1, g2, gg, sg = pl.pallas_call(
        functools.partial(unpack, ch, rows_half),
        out_shape=(
            jax.ShapeDtypeStruct(planes, BF16),
            jax.ShapeDtypeStruct(planes, BF16),
            jax.ShapeDtypeStruct((27 * ch, ch), F32),
            jax.ShapeDtypeStruct((27 * ch, ch), F32),
            jax.ShapeDtypeStruct((1, ch), F32),
            jax.ShapeDtypeStruct((1, ch), F32),
        ),
        in_specs=[vmem] * 4,
        out_specs=[vmem] * 6,
        compiler_params=pltpu.CompilerParams(vmem_limit_bytes=16 * 2**20),
    )(so.reshape(planes), ig.reshape(planes), q4, sums)
    shape = features.shape
    return (so.reshape(shape), ig.reshape(shape), g1.reshape(27, ch, ch),
            g2.reshape(27, ch, ch), gg.reshape(ch), sg.reshape(ch))


def solution(mesh):
    split = P("dp", None, "tile", None)
    return jax.shard_map(
        functools.partial(local, mesh.shape["dp"], mesh.shape["tile"]),
        mesh=mesh,
        in_specs=(split, P("dp", "tile", None), P(), P(), P(), P(), split),
        out_specs=(split, split, P(), P(), P(), P()),
        check_vma=False,
    )
```
